32 devices in a mesh: aux: 16 (over z, x, core), pair: 2 (over y).
Axes of the slice: x: 2, y: 2, z: 4, core: 2. Of those that a mesh axis runs over, the one named last changes fastest.
Arguments:
- three_index: bfloat16 [14336, 512], P('aux', 'pair'), may hold values from -0.375 to 0.375
- occupied_energy: float32 [64], replicated, may hold values from -2 to -0.3
- virtual_energy: float32 [20096], replicated, may hold values from 0.5 to 4
- tile_occupied: int32 [4], replicated, may hold values from 0 to 63
- tile_virtual: int32 [4], replicated, may hold values from 0 to 156
- tile_exponent: int32 [4], replicated, may hold values from -1 to 1
Outputs:
- gamma_terms: bfloat16 [14336, 512], P('aux', 'pair')
The draws below stay inside these ranges and needn't reach their ends.
All inputs are finite; a program needn't handle non-finite values.
Results may differ from the reference program's by a relative error of at most 0.0048.
Values may be sent and summed in bfloat16 or wider, within the bound.
A program may use at most 64 MiB of HBM per device.

```python
import jax
import jax.numpy as jnp

TS = 128
NOCC = 64
VT = 157
NQ = 14336
NVIRT = 20096
NT = 4
NCOL = 512


def plant(values, stream_key, least, largest):
    longest = values.shape.index(max(values.shape))
    spots = []
    for shift in (0, 1):
        where = [jax.random.randint(jax.random.fold_in(stream_key, axis), (), 0, length) for axis, length in enumerate(values.shape)]
        where[longest] = (where[longest] + shift) % values.shape[longest]
        spots.append(tuple(where))
    return values.at[spots[0]].set(least).at[spots[1]].set(largest)


def block_levels(own_key, shape, shards, smallest, high):
    level = 1.0
    for position, parts in shards:
        heights = jax.random.uniform(jax.random.fold_in(jax.random.fold_in(own_key, 6), position), (parts,), jnp.float32, smallest / len(shards), high / len(shards))
        level = level * jnp.repeat(jnp.exp(heights), shape[position] // parts).reshape((-1,) + (1,) * (len(shape) - 1 - position))
    return level


def gaussian(key, extent, scale, bound, shards=(), dtype=jnp.bfloat16):
    level = block_levels(key, extent, shards, -0.22, 0.18) if shards else 1.0
    values = jax.random.normal(key, extent, jnp.float32) * scale * level
    return jnp.minimum(jnp.maximum(values, -bound), bound).astype(dtype)


def setup_inputs(seed: int = 0) -> dict:
    key_of = jax.random.split(jax.random.key(seed), 7)
    return {
        "three_index": gaussian(key_of[0], (NQ, NCOL), (NQ // 64) ** -0.5, 0.375, ((0, 16), (1, 2))),
        "occupied_energy": jnp.clip(jax.random.uniform(key_of[1], (NOCC,), jnp.float32, -2.0, -0.3), -2.0, -0.3),
        "virtual_energy": jnp.clip(jax.random.uniform(key_of[2], (NVIRT,), jnp.float32, 0.5, 4.0), 0.5, 4.0),
        "tile_occupied": plant(jax.random.randint(key_of[3], (NT,), 0, NOCC), jax.random.fold_in(key_of[3], 1), 0, NOCC - 1).astype(jnp.int32),
        "tile_virtual": plant(jax.random.randint(key_of[4], (NT,), 0, VT), jax.random.fold_in(key_of[4], 1), 0, VT - 1).astype(jnp.int32),
        "tile_exponent": plant(jax.random.randint(key_of[5], (NT,), -1, 2), jax.random.fold_in(key_of[5], 1), -1, 1).astype(jnp.int32),
    }


def column_scale(tile_exponent):
    factor = jnp.where(tile_exponent == -1, 0.5, jnp.where(tile_exponent == 1, 2.0, 1.0)).astype(jnp.float32)
    return jnp.repeat(factor, TS)


def column_energy(occupied_energy, virtual_energy, tile_occupied, tile_virtual):
    virtual_cols = virtual_energy.reshape(VT, TS)[tile_virtual].reshape(-1)
    occupied_cols = jnp.repeat(occupied_energy[tile_occupied], TS)
    return virtual_cols - occupied_cols


def reference(three_index, occupied_energy, virtual_energy, tile_occupied, tile_virtual, tile_exponent):
    col_scale = column_scale(tile_exponent)
    col_energy = column_energy(occupied_energy, virtual_energy, tile_occupied, tile_virtual)
    coulomb = jnp.dot(three_index.T, three_index, preferred_element_type=jnp.float32)
    amplitude = (coulomb * (col_scale * col_scale)[:, None] * col_scale[None, :]
                 / (col_energy[:, None] + col_energy[None, :])).astype(jnp.bfloat16)
    return jnp.dot(three_index, amplitude, preferred_element_type=jnp.float32).astype(jnp.bfloat16)
```

```python
import functools

import jax
import jax.numpy as jnp
from jax import lax
from jax.experimental import pallas as pl
from jax.experimental.pallas import tpu as pltpu
from jax.sharding import PartitionSpec as P

TS = 128
VT = 157
F32 = jnp.float32
BF16 = jnp.bfloat16
MESH = pl.DeviceIdType.MESH


def column_scale(tile_exponent):
    factor = jnp.where(tile_exponent == -1, 0.5, jnp.where(tile_exponent == 1, 2.0, 1.0)).astype(
        jnp.float32
    )
    return jnp.repeat(factor, TS)


def column_energy(occupied_energy, virtual_energy, tile_occupied, tile_virtual):
    virtual_cols = virtual_energy.reshape(VT, TS)[tile_virtual].reshape(-1)
    occupied_cols = jnp.repeat(occupied_energy[tile_occupied], TS)
    return virtual_cols - occupied_cols


def make_amplitude(coulomb, row_energy, row_scale, own_energy, own_scale):
    return (
        coulomb
        * (row_scale * row_scale)[:, None]
        * own_scale[None, :]
        / (row_energy[:, None] + own_energy[None, :])
    ).astype(jnp.bfloat16)


def general_body(
    three_index, occupied_energy, virtual_energy, tile_occupied, tile_virtual, tile_exponent
):
    width_local = three_index.shape[1]
    col_scale = column_scale(tile_exponent)
    col_energy = column_energy(occupied_energy, virtual_energy, tile_occupied, tile_virtual)
    offset = lax.axis_index("pair") * width_local
    own_energy = lax.dynamic_slice_in_dim(col_energy, offset, width_local)
    own_scale = lax.dynamic_slice_in_dim(col_scale, offset, width_local)
    contract = (((0,), (0,)), ((), ()))
    gathered = lax.all_gather(three_index, "pair", axis=1, tiled=True)
    coulomb = lax.dot_general(gathered, three_index, contract, preferred_element_type=jnp.float32)
    summed = lax.psum(coulomb, "aux")
    amplitude = make_amplitude(summed, col_energy, col_scale, own_energy, own_scale)
    result = jnp.dot(gathered, amplitude, preferred_element_type=jnp.float32)
    return result.astype(jnp.bfloat16)


def tn_dot(a, b):
    return lax.dot_general(a, b, (((0,), (0,)), ((), ())), preferred_element_type=F32)


def nt_dot(a, b):
    return lax.dot_general(a, b, (((1,), (1,)), ((), ())), preferred_element_type=F32)


def nn_dot(a, b):
    return jnp.dot(a, b, preferred_element_type=F32)


def kernel(
    Q, b_ref, ve_ref, occ_ref, to_ref, tv_ref, te_ref, out_ref,
    other, own_c, off_c, own_core, off_core, own_part, off_part, own_got, off_got,
    own_amp, off_amp, stage, energy,
    b_s, b_r, core_s, core_r, own_s, own_r, off_s, off_r, owna_s, owna_r, offa_s, offa_r, fw_s, fw_r,
):
    rows = b_ref.shape[0]
    half = rows // 2
    piece = TS // Q
    aux = lax.axis_index("aux")
    j = lax.axis_index("pair")
    core = lax.rem(aux, 2)
    q = lax.div(aux, 2)
    G = 2 * Q
    g = j * Q + q

    def dev(chip, which):
        return {"aux": 2 * lax.rem(chip, Q) + which, "pair": lax.div(chip, Q)}

    def remote(src, dst, send, recv, target):
        return pltpu.make_async_remote_copy(
            src_ref=src, dst_ref=dst, send_sem=send, recv_sem=recv,
            device_id=target, device_id_type=MESH,
        )

    def others(n, me, f):
        def step(i, carry):
            f(lax.rem(me + i, n))
            return carry
        lax.fori_loop(1, n, step, 0)

    sibling = dev(g, 1 - core)
    across = dev(lax.rem(g + Q, G), core)

    barrier = pltpu.get_barrier_semaphore()
    pl.semaphore_signal(barrier, inc=1, device_id=sibling, device_id_type=MESH)
    others(G, g, lambda t: pl.semaphore_signal(
        barrier, inc=1, device_id=dev(t, core), device_id_type=MESH))

    for t in range(4):
        energy[t:t + 1, :] = ve_ref[pl.ds(tv_ref[t], 1), :] - occ_ref[to_ref[t]]
    own_c[...] = tn_dot(b_ref[...], b_ref[...])
    pl.semaphore_wait(barrier, G)

    mine = pl.multiple_of(core * TS, TS)
    theirs = pl.multiple_of((1 - core) * TS, TS)
    at_q = pl.multiple_of(q * piece, piece)

    def send_b(k):
        first = pl.multiple_of((j if k == 0 else 1 - j) * half, half)
        return remote(b_ref.at[pl.ds(first, half)], other.at[pl.ds(first, half)],
                      b_s.at[k], b_r.at[k], across)

    def got_b(k):
        first = pl.multiple_of((1 - j if k == 0 else j) * half, half)
        return remote(b_ref.at[pl.ds(first, half)], other.at[pl.ds(first, half)],
                      b_s.at[k], b_r.at[k], across)

    def core_copy(k, src, dst):
        return remote(src.at[pl.ds(theirs, TS)], dst, core_s.at[k], core_r.at[k], sibling)

    send_b(0).start()
    core_copy(0, own_c, own_core).start()
    core_copy(0, own_c, own_core).wait_recv()
    own_core[...] += own_c[pl.ds(mine, TS), :]
    own_part[...] = own_core[...].astype(BF16)

    def own_scatter(t):
        return remote(own_part.at[pl.ds(pl.multiple_of(t * piece, piece), piece)], own_got.at[q],
                      own_s.at[t], own_r.at[q], dev(j * Q + t, core))

    def own_arrival(p):
        return remote(own_part.at[pl.ds(0, piece)], own_got.at[p],
                      own_s.at[p], own_r.at[p], dev(j * Q + p, core))

    others(Q, q, lambda t: own_scatter(t).start())

    got_b(0).wait_recv()
    send_b(0).wait_send()
    send_b(1).start()
    here = pl.multiple_of((1 - j) * half, half)

    @pl.when(j == 0)
    def _():
        off_c[...] = tn_dot(b_ref[pl.ds(here, half), :], other[pl.ds(here, half), :])

    @pl.when(j == 1)
    def _():
        off_c[...] = tn_dot(other[pl.ds(here, half), :], b_ref[pl.ds(here, half), :])

    core_copy(1, off_c, off_core).start()

    def scale(t):
        e = te_ref[t]
        return jnp.where(e == -1, 0.5, jnp.where(e == 1, 2.0, 1.0)).astype(F32)

    def down(row):
        shape = (piece, TS)
        pick = lax.broadcasted_iota(jnp.int32, shape, 1) == (
            lax.broadcasted_iota(jnp.int32, shape, 0) + q * piece)
        return jnp.sum(jnp.where(pick, row, 0.0), axis=1, keepdims=True)

    def add_own(i, total):
        p = lax.rem(q + i, Q)
        own_arrival(p).wait_recv()
        return total + own_got[p].astype(F32)

    own_total = lax.fori_loop(1, Q, add_own, own_core[pl.ds(at_q, piece), :])
    own_rows = pl.ds(pl.multiple_of(core * TS + q * piece, piece), piece)
    row_e = down(energy[pl.ds(2 * j + core, 1), :])
    row_s = scale(2 * j + core)
    for h in range(2):
        col_e = energy[pl.ds(2 * j + h, 1), :]
        col_s = scale(2 * j + h)
        own_amp[own_rows, h * TS:(h + 1) * TS] = (
            own_total[:, h * TS:(h + 1) * TS] * (row_s * row_s) * col_s / (row_e + col_e)
        ).astype(BF16)

    def own_gather(t):
        return remote(own_amp.at[own_rows], own_amp.at[own_rows],
                      owna_s.at[t], owna_r.at[q], dev(j * Q + t, core))

    def own_gathered(p):
        place = own_amp.at[pl.ds(pl.multiple_of(core * TS + p * piece, piece), piece)]
        return remote(place, place, owna_s.at[p], owna_r.at[p], dev(j * Q + p, core))

    others(Q, q, lambda t: own_gather(t).start())

    core_copy(1, off_c, off_core).wait_recv()
    off_core[...] += off_c[pl.ds(mine, TS), :]
    for h in range(2):
        off_part[h] = off_core[:, h * TS:(h + 1) * TS].astype(BF16)

    def off_scatter(t):
        at = pl.multiple_of(lax.rem(t, Q) * piece, piece)
        return remote(off_part.at[lax.div(t, Q), pl.ds(at, piece)], off_got.at[g],
                      off_s.at[t], off_r.at[g], dev(t, core))

    def off_arrival(p):
        return remote(off_part.at[0, pl.ds(0, piece)], off_got.at[p],
                      off_s.at[p], off_r.at[p], dev(p, core))

    others(G, g, lambda t: off_scatter(t).start())

    others(Q, q, lambda p: own_gathered(p).wait_recv())

    def own_forward(first):
        place = own_amp.at[pl.ds(first, TS)]
        return remote(place, place, fw_s.at[0], fw_r.at[0], sibling)

    own_forward(mine).start()

    def add_off(i, total):
        p = lax.rem(g + i, G)
        off_arrival(p).wait_recv()
        return total + off_got[p].astype(F32)

    off_mine = off_core[pl.ds(at_q, piece), pl.ds(pl.multiple_of(j * TS, TS), TS)]
    off_total = lax.fori_loop(1, G, add_off, off_mine)
    row_e = down(energy[pl.ds(core, 1), :])
    row_s = scale(core)
    col_e = energy[pl.ds(2 + j, 1), :]
    col_s = scale(2 + j)
    denominator = row_e + col_e
    stage[0] = (off_total * (col_s * col_s) * row_s / denominator).astype(BF16)
    stage[1] = (off_total * (row_s * row_s) * col_s / denominator).astype(BF16)

    def off_gather(t):
        return remote(stage.at[lax.div(t, Q)], off_amp.at[j, own_rows],
                      offa_s.at[t], offa_r.at[g], dev(t, core))

    def off_gathered(p):
        at = pl.multiple_of(core * TS + lax.rem(p, Q) * piece, piece)
        return remote(stage.at[0], off_amp.at[lax.div(p, Q), pl.ds(at, piece)],
                      offa_s.at[p], offa_r.at[p], dev(p, core))

    others(G, g, lambda t: off_gather(t).start())
    off_amp[j, own_rows, :] = stage[j]

    others(G, g, lambda p: off_gathered(p).wait_recv())

    def off_forward(h, first):
        place = off_amp.at[h, pl.ds(first, TS)]
        return remote(place, place, fw_s.at[1 + h], fw_r.at[1 + h], sibling)

    for h in range(2):
        off_forward(h, mine).start()
    own_forward(theirs).wait_recv()
    got_b(1).wait_recv()
    for h in range(2):
        off_forward(h, theirs).wait_recv()

    @pl.when(j == 0)
    def _():
        out_ref[...] = (nn_dot(b_ref[...], own_amp[...])
                        + nt_dot(other[:, :TS], off_amp[0])
                        + nt_dot(other[:, TS:], off_amp[1])).astype(BF16)

    @pl.when(j == 1)
    def _():
        for h in range(2):
            cols = slice(h * TS, (h + 1) * TS)
            out_ref[:, cols] = (nn_dot(b_ref[...], own_amp[:, cols])
                                + nn_dot(other[...], off_amp[h])).astype(BF16)

    send_b(1).wait_send()
    core_copy(0, own_c, own_core).wait_send()
    core_copy(1, off_c, off_core).wait_send()
    others(Q, q, lambda t: own_scatter(t).wait_send())
    others(Q, q, lambda t: own_gather(t).wait_send())
    others(G, g, lambda t: off_scatter(t).wait_send())
    others(G, g, lambda t: off_gather(t).wait_send())
    own_forward(mine).wait_send()
    for h in range(2):
        off_forward(h, mine).wait_send()


def pair_body(Q, three_index, occupied_energy, virtual_energy, tile_occupied, tile_virtual,
              tile_exponent):
    rows, width = three_index.shape
    piece = TS // Q
    G = 2 * Q
    vmem = pl.BlockSpec(memory_space=pltpu.VMEM)
    smem = pl.BlockSpec(memory_space=pltpu.SMEM)
    dma = pltpu.SemaphoreType.DMA
    flops = 2 * rows * width * width * 4
    return pl.pallas_call(
        functools.partial(kernel, Q),
        out_shape=jax.ShapeDtypeStruct((rows, width), BF16),
        in_specs=[vmem, vmem, smem, smem, smem, smem],
        out_specs=vmem,
        scratch_shapes=[
            pltpu.VMEM((rows, width), BF16),
            pltpu.VMEM((width, width), F32),
            pltpu.VMEM((width, width), F32),
            pltpu.VMEM((TS, width), F32),
            pltpu.VMEM((TS, width), F32),
            pltpu.VMEM((TS, width), BF16),
            pltpu.VMEM((2, TS, TS), BF16),
            pltpu.VMEM((Q, piece, width), BF16),
            pltpu.VMEM((G, piece, TS), BF16),
            pltpu.VMEM((width, width), BF16),
            pltpu.VMEM((2, width, TS), BF16),
            pltpu.VMEM((2, piece, TS), BF16),
            pltpu.VMEM((8, TS), F32),
            dma((2,)), dma((2,)),
            dma((2,)), dma((2,)),
            dma((Q,)), dma((Q,)),
            dma((G,)), dma((G,)),
            dma((Q,)), dma((Q,)),
            dma((G,)), dma((G,)),
            dma((3,)), dma((3,)),
        ],
        compiler_params=pltpu.CompilerParams(
            collective_id=0, has_side_effects=True, vmem_limit_bytes=32 * 1024 * 1024
        ),
        cost_estimate=pl.CostEstimate(
            flops=flops, bytes_accessed=4 * rows * width, transcendentals=0
        ),
    )(three_index, virtual_energy.reshape(VT, TS), occupied_energy, tile_occupied, tile_virtual,
      tile_exponent)


def solution(mesh):
    placed = (P("aux", "pair"), P(), P(), P(), P(), P())
    Q = mesh.shape["aux"] // 2

    def body(*args):
        if mesh.shape["pair"] == 2 and Q == 8 and args[0].shape[1] == 2 * TS:
            return pair_body(Q, *args)
        return general_body(*args)

    return jax.shard_map(
        body, mesh=mesh, in_specs=placed, out_specs=P("aux", "pair"), check_vma=False
    )
```

```python
import functools

import jax
import jax.numpy as jnp
from jax import lax
from jax.experimental import pallas as pl
from jax.experimental.pallas import tpu as pltpu
from jax.sharding import PartitionSpec as P

TS = 128
VT = 157
F32 = jnp.float32
BF16 = jnp.bfloat16
MESH = pl.DeviceIdType.MESH
VMEM_LIMIT = 60 * 1024 * 1024


def column_scale(tile_exponent):
    factor = jnp.where(tile_exponent == -1, 0.5, jnp.where(tile_exponent == 1, 2.0, 1.0)).astype(
        jnp.float32
    )
    return jnp.repeat(factor, TS)


def column_energy(occupied_energy, virtual_energy, tile_occupied, tile_virtual):
    virtual_cols = virtual_energy.reshape(VT, TS)[tile_virtual].reshape(-1)
    occupied_cols = jnp.repeat(occupied_energy[tile_occupied], TS)
    return virtual_cols - occupied_cols


def make_amplitude(coulomb, row_energy, row_scale, own_energy, own_scale):
    return (
        coulomb
        * (row_scale * row_scale)[:, None]
        * own_scale[None, :]
        / (row_energy[:, None] + own_energy[None, :])
    ).astype(jnp.bfloat16)


def general_body(
    three_index, occupied_energy, virtual_energy, tile_occupied, tile_virtual, tile_exponent
):
    width_local = three_index.shape[1]
    col_scale = column_scale(tile_exponent)
    col_energy = column_energy(occupied_energy, virtual_energy, tile_occupied, tile_virtual)
    offset = lax.axis_index("pair") * width_local
    own_energy = lax.dynamic_slice_in_dim(col_energy, offset, width_local)
    own_scale = lax.dynamic_slice_in_dim(col_scale, offset, width_local)
    contract = (((0,), (0,)), ((), ()))
    gathered = lax.all_gather(three_index, "pair", axis=1, tiled=True)
    coulomb = lax.dot_general(gathered, three_index, contract, preferred_element_type=jnp.float32)
    summed = lax.psum(coulomb, "aux")
    amplitude = make_amplitude(summed, col_energy, col_scale, own_energy, own_scale)
    result = jnp.dot(gathered, amplitude, preferred_element_type=jnp.float32)
    return result.astype(jnp.bfloat16)


def tn_dot(a, b):
    return lax.dot_general(a, b, (((0,), (0,)), ((), ())), preferred_element_type=F32)


def nt_dot(a, b):
    return lax.dot_general(a, b, (((1,), (1,)), ((), ())), preferred_element_type=F32)


def nn_dot(a, b):
    return jnp.dot(a, b, preferred_element_type=F32)


def kernel(
    Q, b_hbm, ve_hbm, occ_hbm, to_hbm, tv_hbm, te_hbm, out_ref,
    b_ref, ve_ref, occ_ref, to_ref, tv_ref, te_ref,
    other, own_send, own_sum, own_core, off_send, off_sum, off_core, own_part, off_part,
    own_got, off_got, own_amp, off_amp, stage, energy,
    load, b_s, b_r, core_s, core_r, own_s, own_r, off_s, off_r, owna_s, owna_r, offa_s, offa_r,
    fw_s, fw_r,
):
    rows = b_ref.shape[0]
    half = rows // 2
    piece = TS // Q
    aux = lax.axis_index("aux")
    j = lax.axis_index("pair")
    core = lax.rem(aux, 2)
    q = lax.div(aux, 2)
    G = 2 * Q
    g = j * Q + q

    def dev(chip, which):
        return {"aux": 2 * lax.rem(chip, Q) + which, "pair": lax.div(chip, Q)}

    def remote(src, dst, send, recv, target):
        return pltpu.make_async_remote_copy(
            src_ref=src, dst_ref=dst, send_sem=send, recv_sem=recv,
            device_id=target, device_id_type=MESH,
        )

    sibling = dev(g, 1 - core)
    across = dev(lax.rem(g + Q, G), core)
    chips = [lax.rem(g + i, G) for i in range(1, G)]
    own_chips = [lax.rem(q + i, Q) for i in range(1, Q)]

    loads = [
        pltpu.make_async_copy(src, dst, load.at[k])
        for k, (src, dst) in enumerate([
            (b_hbm, b_ref), (ve_hbm, ve_ref), (occ_hbm, occ_ref),
            (to_hbm, to_ref), (tv_hbm, tv_ref), (te_hbm, te_ref),
        ])
    ]
    barrier = pltpu.get_barrier_semaphore()
    pl.semaphore_signal(barrier, inc=1, device_id=sibling, device_id_type=MESH)
    for t in chips:
        pl.semaphore_signal(barrier, inc=1, device_id=dev(t, core), device_id_type=MESH)
    for one in loads:
        one.start()

    mine = pl.multiple_of(core * TS, TS)
    theirs = pl.multiple_of((1 - core) * TS, TS)
    at_q = pl.multiple_of(q * piece, piece)
    own_rows = pl.ds(pl.multiple_of(core * TS + q * piece, piece), piece)
    here = pl.multiple_of((1 - j) * half, half)
    away = pl.multiple_of(j * half, half)
    half_rows = [(away, here), (here, away)]

    def send_b(k):
        at = pl.ds(half_rows[k][0], half)
        return remote(b_hbm.at[at], other.at[at], b_s.at[k], b_r.at[k], across)

    def got_b(k):
        at = pl.ds(half_rows[k][1], half)
        return remote(b_hbm.at[at], other.at[at], b_s.at[k], b_r.at[k], across)

    pl.semaphore_wait(barrier, G)
    send_b(0).start()

    own_core_copy = remote(own_send, own_core, core_s.at[0], core_r.at[0], sibling)
    loads[0].wait()
    own_send[...] = tn_dot(b_ref[:, pl.ds(theirs, TS)], b_ref[...])
    own_core_copy.start()
    own_sum[...] = tn_dot(b_ref[:, pl.ds(mine, TS)], b_ref[...])

    for one in loads[1:]:
        one.wait()
    for t in range(4):
        energy[t:t + 1, :] = ve_ref[pl.ds(tv_ref[t], 1), :] - occ_ref[to_ref[t]]

    def scale(t):
        e = te_ref[t]
        return jnp.where(e == -1, 0.5, jnp.where(e == 1, 2.0, 1.0)).astype(F32)

    def down(row):
        shape = (piece, TS)
        pick = lax.broadcasted_iota(jnp.int32, shape, 1) == (
            lax.broadcasted_iota(jnp.int32, shape, 0) + q * piece)
        return jnp.sum(jnp.where(pick, row, 0.0), axis=1, keepdims=True)

    own_got[q] = jnp.zeros(own_got.shape[1:], BF16)
    off_got[g] = jnp.zeros(off_got.shape[1:], BF16)

    own_core_copy.wait_recv()
    own_sum[...] += own_core[...]
    own_part[...] = own_sum[...].astype(BF16)
    for t in own_chips:
        remote(own_part.at[pl.ds(pl.multiple_of(t * piece, piece), piece)], own_got.at[q],
               own_s, own_r, dev(j * Q + t, core)).start()

    own_bytes = own_got.at[pl.ds(0, Q - 1)]
    own_all = remote(own_bytes, own_bytes, own_s, own_r, sibling)
    own_all.wait_recv()
    own_total = own_sum[pl.ds(at_q, piece), :]
    for p in range(Q):
        own_total = own_total + own_got[p].astype(F32)
    row_e = down(energy[pl.ds(2 * j + core, 1), :])
    row_s = scale(2 * j + core)
    for h in range(2):
        cols = slice(h * TS, (h + 1) * TS)
        col_e = energy[pl.ds(2 * j + h, 1), :]
        col_s = scale(2 * j + h)
        own_amp[own_rows, cols] = (
            own_total[:, cols] * (row_s * row_s) * col_s / (row_e + col_e)
        ).astype(BF16)
    for t in own_chips:
        remote(own_amp.at[own_rows], own_amp.at[own_rows],
               owna_s, owna_r, dev(j * Q + t, core)).start()

    off_core_copy = remote(off_send, off_core, core_s.at[1], core_r.at[1], sibling)
    here_rows = pl.ds(here, half)
    got_b(0).wait_recv()

    @pl.when(j == 0)
    def _():
        off_send[...] = tn_dot(b_ref[here_rows, pl.ds(theirs, TS)], other[here_rows, :])

    @pl.when(j == 1)
    def _():
        off_send[...] = tn_dot(other[here_rows, pl.ds(theirs, TS)], b_ref[here_rows, :])

    off_core_copy.start()

    @pl.when(j == 0)
    def _():
        off_sum[...] = tn_dot(b_ref[here_rows, pl.ds(mine, TS)], other[here_rows, :])

    @pl.when(j == 1)
    def _():
        off_sum[...] = tn_dot(other[here_rows, pl.ds(mine, TS)], b_ref[here_rows, :])

    off_core_copy.wait_recv()
    off_sum[...] += off_core[...]
    for h in range(2):
        off_part[h] = off_sum[:, h * TS:(h + 1) * TS].astype(BF16)
    for t in chips:
        at = pl.multiple_of(lax.rem(t, Q) * piece, piece)
        remote(off_part.at[lax.div(t, Q), pl.ds(at, piece)], off_got.at[g],
               off_s, off_r, dev(t, core)).start()
    send_b(0).wait_send()
    send_b(1).start()

    own_amp_bytes = own_amp.at[pl.ds(0, (Q - 1) * piece)]
    own_amp_all = remote(own_amp_bytes, own_amp_bytes, owna_s, owna_r, sibling)
    own_amp_all.wait_recv()

    def own_forward(first):
        place = own_amp.at[pl.ds(first, TS)]
        return remote(place, place, fw_s.at[0], fw_r.at[0], sibling)

    own_forward(mine).start()
    own_core_copy.wait_send()
    own_all.wait_send()
    own_amp_all.wait_send()

    row_e = down(energy[pl.ds(core, 1), :])
    row_s = scale(core)
    col_e = energy[pl.ds(2 + j, 1), :]
    col_s = scale(2 + j)
    denominator = row_e + col_e
    off_bytes = off_got.at[pl.ds(0, G - 1)]
    off_all = remote(off_bytes, off_bytes, off_s, off_r, sibling)
    off_all.wait_recv()
    off_total = off_sum[pl.ds(at_q, piece), pl.ds(pl.multiple_of(j * TS, TS), TS)]
    for p in range(G):
        off_total = off_total + off_got[p].astype(F32)
    stage[0] = (off_total * (col_s * col_s) * row_s / denominator).astype(BF16)
    stage[1] = (off_total * (row_s * row_s) * col_s / denominator).astype(BF16)
    for t in chips:
        remote(stage.at[lax.div(t, Q)], off_amp.at[j, own_rows],
               offa_s, offa_r, dev(t, core)).start()
    off_amp[j, own_rows, :] = stage[j]
    off_core_copy.wait_send()
    off_all.wait_send()

    off_amp_bytes = off_amp.at[0, pl.ds(0, (G - 1) * piece)]
    off_amp_all = remote(off_amp_bytes, off_amp_bytes, offa_s, offa_r, sibling)
    off_amp_all.wait_recv()

    def off_forward(h, first):
        place = off_amp.at[h, pl.ds(first, TS)]
        return remote(place, place, fw_s.at[1 + h], fw_r.at[1 + h], sibling)

    for h in range(2):
        off_forward(h, mine).start()
    off_amp_all.wait_send()
    own_forward(mine).wait_send()
    own_forward(theirs).wait_recv()
    send_b(1).wait_send()
    got_b(1).wait_recv()
    for h in range(2):
        off_forward(h, theirs).wait_recv()

    @pl.when(j == 0)
    def _():
        out_ref[...] = (nn_dot(b_ref[...], own_amp[...])
                        + nt_dot(other[:, :TS], off_amp[0])
                        + nt_dot(other[:, TS:], off_amp[1])).astype(BF16)

    @pl.when(j == 1)
    def _():
        for h in range(2):
            cols = slice(h * TS, (h + 1) * TS)
            out_ref[:, cols] = (nn_dot(b_ref[...], own_amp[:, cols])
                                + nn_dot(other[...], off_amp[h])).astype(BF16)

    for h in range(2):
        off_forward(h, mine).wait_send()


def pair_body(Q, three_index, occupied_energy, virtual_energy, tile_occupied, tile_virtual,
              tile_exponent):
    rows, width = three_index.shape
    piece = TS // Q
    G = 2 * Q
    hbm = pl.BlockSpec(memory_space=pl.ANY)
    dma = pltpu.SemaphoreType.DMA
    flops = 2 * rows * width * width * 4
    return pl.pallas_call(
        functools.partial(kernel, Q),
        out_shape=jax.ShapeDtypeStruct((rows, width), BF16),
        in_specs=[hbm] * 6,
        out_specs=pl.BlockSpec(memory_space=pltpu.VMEM),
        scratch_shapes=[
            pltpu.VMEM((rows, width), BF16),
            pltpu.VMEM((VT, TS), F32),
            pltpu.SMEM(occupied_energy.shape, F32),
            pltpu.SMEM(tile_occupied.shape, jnp.int32),
            pltpu.SMEM(tile_virtual.shape, jnp.int32),
            pltpu.SMEM(tile_exponent.shape, jnp.int32),
            pltpu.VMEM((rows, width), BF16),
            pltpu.VMEM((TS, width), F32),
            pltpu.VMEM((TS, width), F32),
            pltpu.VMEM((TS, width), F32),
            pltpu.VMEM((TS, width), F32),
            pltpu.VMEM((TS, width), F32),
            pltpu.VMEM((TS, width), F32),
            pltpu.VMEM((TS, width), BF16),
            pltpu.VMEM((2, TS, TS), BF16),
            pltpu.VMEM((Q, piece, width), BF16),
            pltpu.VMEM((G, piece, TS), BF16),
            pltpu.VMEM((width, width), BF16),
            pltpu.VMEM((2, width, TS), BF16),
            pltpu.VMEM((2, piece, TS), BF16),
            pltpu.VMEM((8, TS), F32),
            dma((6,)),
            dma((2,)), dma((2,)),
            dma((2,)), dma((2,)),
            dma, dma, dma, dma, dma, dma, dma, dma,
            dma((3,)), dma((3,)),
        ],
        compiler_params=pltpu.CompilerParams(
            collective_id=0, has_side_effects=True, vmem_limit_bytes=VMEM_LIMIT
        ),
        cost_estimate=pl.CostEstimate(
            flops=flops, bytes_accessed=4 * rows * width, transcendentals=0
        ),
    )(three_index, virtual_energy.reshape(VT, TS), occupied_energy, tile_occupied, tile_virtual,
      tile_exponent)


def solution(mesh):
    placed = (P("aux", "pair"), P(), P(), P(), P(), P())
    Q = mesh.shape["aux"] // 2

    def body(*args):
        if mesh.shape["pair"] == 2 and Q == 8 and args[0].shape[1] == 2 * TS:
            return pair_body(Q, *args)
        return general_body(*args)

    return jax.shard_map(
        body, mesh=mesh, in_specs=placed, out_specs=P("aux", "pair"), check_vma=False
    )
```

```python
import functools

import jax
import jax.numpy as jnp
from jax import lax
from jax.experimental import pallas as pl
from jax.experimental.pallas import tpu as pltpu
from jax.sharding import PartitionSpec as P

TS = 128
VT = 157
F32 = jnp.float32
BF16 = jnp.bfloat16
MESH = pl.DeviceIdType.MESH
VMEM_LIMIT = 60 * 1024 * 1024


def column_scale(tile_exponent):
    factor = jnp.where(tile_exponent == -1, 0.5, jnp.where(tile_exponent == 1, 2.0, 1.0)).astype(
        jnp.float32
    )
    return jnp.repeat(factor, TS)


def column_energy(occupied_energy, virtual_energy, tile_occupied, tile_virtual):
    virtual_cols = virtual_energy.reshape(VT, TS)[tile_virtual].reshape(-1)
    occupied_cols = jnp.repeat(occupied_energy[tile_occupied], TS)
    return virtual_cols - occupied_cols


def make_amplitude(coulomb, row_energy, row_scale, own_energy, own_scale):
    return (
        coulomb
        * (row_scale * row_scale)[:, None]
        * own_scale[None, :]
        / (row_energy[:, None] + own_energy[None, :])
    ).astype(jnp.bfloat16)


def general_body(
    three_index, occupied_energy, virtual_energy, tile_occupied, tile_virtual, tile_exponent
):
    width_local = three_index.shape[1]
    col_scale = column_scale(tile_exponent)
    col_energy = column_energy(occupied_energy, virtual_energy, tile_occupied, tile_virtual)
    offset = lax.axis_index("pair") * width_local
    own_energy = lax.dynamic_slice_in_dim(col_energy, offset, width_local)
    own_scale = lax.dynamic_slice_in_dim(col_scale, offset, width_local)
    contract = (((0,), (0,)), ((), ()))
    gathered = lax.all_gather(three_index, "pair", axis=1, tiled=True)
    coulomb = lax.dot_general(gathered, three_index, contract, preferred_element_type=jnp.float32)
    summed = lax.psum(coulomb, "aux")
    amplitude = make_amplitude(summed, col_energy, col_scale, own_energy, own_scale)
    result = jnp.dot(gathered, amplitude, preferred_element_type=jnp.float32)
    return result.astype(jnp.bfloat16)


def tn_dot(a, b):
    return lax.dot_general(a, b, (((0,), (0,)), ((), ())), preferred_element_type=F32)


def nt_dot(a, b):
    return lax.dot_general(a, b, (((1,), (1,)), ((), ())), preferred_element_type=F32)


def nn_dot(a, b):
    return jnp.dot(a, b, preferred_element_type=F32)


def kernel(
    W, Z, b_hbm, ve_hbm, occ_hbm, to_hbm, tv_hbm, te_hbm, total_ref, other, off_amp,
    b_ref, ve_ref, occ_ref, to_ref, tv_ref, te_ref,
    own_sum, off_sum, own_part, off_part, own_got, off_got, own_line, off_line,
    own_line_got, off_line_got, own_amp, stage, energy,
    load, b_s, b_r, sems,
):
    rows, width = b_ref.shape
    half = rows // 2
    S = 2 * W
    own_piece = width // W
    off_piece = width // S
    aux = lax.axis_index("aux")
    j = lax.axis_index("pair")
    z = lax.div(aux, W)
    w = lax.rem(aux, W)
    s = j * W + w

    def dev(line, place):
        return {"aux": line * W + lax.rem(place, W), "pair": lax.div(place, W)}

    def remote(src, dst, send, recv, target):
        return pltpu.make_async_remote_copy(
            src_ref=src, dst_ref=dst, send_sem=send, recv_sem=recv,
            device_id=target, device_id_type=MESH,
        )

    across = dev(z, lax.rem(s + W, S))
    plane = [lax.rem(s + i, S) for i in range(1, S)]
    side = [lax.rem(w + i, W) for i in range(1, W)]
    line = [lax.rem(z + i, Z) for i in range(1, Z)]

    loads = [
        pltpu.make_async_copy(src, dst, load.at[k])
        for k, (src, dst) in enumerate([
            (b_hbm, b_ref), (ve_hbm, ve_ref), (occ_hbm, occ_ref),
            (to_hbm, to_ref), (tv_hbm, tv_ref), (te_hbm, te_ref),
        ])
    ]
    barrier = pltpu.get_barrier_semaphore()
    for k in plane:
        pl.semaphore_signal(barrier, inc=1, device_id=dev(z, k), device_id_type=MESH)
    for k in line:
        pl.semaphore_signal(barrier, inc=1, device_id=dev(k, s), device_id_type=MESH)
    for one in loads:
        one.start()

    here = pl.multiple_of((1 - j) * half, half)
    away = pl.multiple_of(j * half, half)
    half_rows = [(away, here), (here, away)]
    own_at = pl.multiple_of(w * own_piece, own_piece)
    off_at = pl.multiple_of(s * off_piece, off_piece)

    def send_b(k):
        at = pl.ds(half_rows[k][0], half)
        return remote(b_hbm.at[at], other.at[at], b_s.at[k], b_r.at[k], across)

    def got_b(k):
        at = pl.ds(half_rows[k][1], half)
        return remote(b_hbm.at[at], other.at[at], b_s.at[k], b_r.at[k], across)

    def group(k, ref):
        return remote(ref, ref, sems.at[2 * k], sems.at[2 * k + 1], across)

    def scale(t):
        e = te_ref[t]
        return jnp.where(e == -1, 0.5, jnp.where(e == 1, 2.0, 1.0)).astype(F32)

    def down(row, first, count):
        shape = (count, TS)
        pick = lax.broadcasted_iota(jnp.int32, shape, 1) == (
            lax.broadcasted_iota(jnp.int32, shape, 0) + first)
        return jnp.sum(jnp.where(pick, row, 0.0), axis=1, keepdims=True)

    pl.semaphore_wait(barrier, S - 1 + Z - 1)
    send_b(0).start()

    loads[0].wait()
    own_sum[...] = tn_dot(b_ref[...], b_ref[...])
    own_part[...] = own_sum[...].astype(BF16)
    for k in side:
        remote(own_part.at[pl.ds(pl.multiple_of(k * own_piece, own_piece), own_piece)],
               own_got.at[w], sems.at[0], sems.at[1], dev(z, j * W + k)).start()

    for one in loads[1:]:
        one.wait()
    for t in range(4):
        energy[t:t + 1, :] = ve_ref[pl.ds(tv_ref[t], 1), :] - occ_ref[to_ref[t]]
    own_got[w] = jnp.zeros(own_got.shape[1:], BF16)
    off_got[s] = jnp.zeros(off_got.shape[1:], BF16)
    own_line_got[z] = jnp.zeros(own_line_got.shape[1:], BF16)
    off_line_got[z] = jnp.zeros(off_line_got.shape[1:], BF16)

    own_scattered = group(0, own_got.at[pl.ds(0, W - 1)])
    own_scattered.wait_recv()
    own_total = own_sum[pl.ds(own_at, own_piece), :]
    for k in range(W):
        own_total = own_total + own_got[k].astype(F32)
    own_line[...] = own_total.astype(BF16)
    for k in line:
        remote(own_line, own_line_got.at[z], sems.at[2], sems.at[3], dev(k, s)).start()

    here_rows = pl.ds(here, half)
    got_b(0).wait_recv()

    @pl.when(j == 0)
    def _():
        off_sum[...] = tn_dot(b_ref[here_rows, :], other[here_rows, :])

    @pl.when(j == 1)
    def _():
        off_sum[...] = tn_dot(other[here_rows, :], b_ref[here_rows, :])

    off_part[...] = off_sum[...].astype(BF16)
    for k in plane:
        remote(off_part.at[pl.ds(pl.multiple_of(k * off_piece, off_piece), off_piece)],
               off_got.at[s], sems.at[6], sems.at[7], dev(z, k)).start()
    send_b(0).wait_send()
    send_b(1).start()

    own_lined = group(1, own_line_got.at[pl.ds(0, Z - 1)])
    own_lined.wait_recv()
    for k in range(Z):
        own_total = own_total + own_line_got[k].astype(F32)
    tile = lax.div(own_at, TS)
    row_e = down(energy[pl.ds(2 * j + tile, 1), :], lax.rem(own_at, TS), own_piece)
    row_s = scale(2 * j + tile)
    own_rows = pl.ds(own_at, own_piece)
    for h in range(2):
        cols = slice(h * TS, (h + 1) * TS)
        col_e = energy[pl.ds(2 * j + h, 1), :]
        col_s = scale(2 * j + h)
        own_amp[own_rows, cols] = (
            own_total[:, cols] * (row_s * row_s) * col_s / (row_e + col_e)
        ).astype(BF16)
    for k in side:
        remote(own_amp.at[own_rows], own_amp.at[own_rows],
               sems.at[4], sems.at[5], dev(z, j * W + k)).start()

    off_scattered = group(3, off_got.at[pl.ds(0, S - 1)])
    off_scattered.wait_recv()
    off_total = off_sum[pl.ds(off_at, off_piece), :]
    for k in range(S):
        off_total = off_total + off_got[k].astype(F32)
    off_line[...] = off_total.astype(BF16)
    for k in line:
        remote(off_line, off_line_got.at[z], sems.at[8], sems.at[9], dev(k, s)).start()

    own_gathered = group(2, own_amp.at[pl.ds(0, (W - 1) * own_piece)])
    own_gathered.wait_recv()
    total_ref[...] = nn_dot(b_ref[...], own_amp[...])
    own_scattered.wait_send()
    own_lined.wait_send()
    off_scattered.wait_send()

    row_e = down(energy[pl.ds(j, 1), :], w * off_piece, off_piece)
    row_s = scale(j)
    off_lined = group(4, off_line_got.at[pl.ds(0, Z - 1)])
    off_lined.wait_recv()
    for k in range(Z):
        off_total = off_total + off_line_got[k].astype(F32)
    for h in range(2):
        cols = slice(h * TS, (h + 1) * TS)
        denominator = row_e + energy[2 + h:3 + h, :]
        col_s = scale(2 + h)
        value = off_total[:, cols]
        stage[0, :, cols] = (value * (col_s * col_s) * row_s / denominator).astype(BF16)
        stage[1, :, cols] = (value * (row_s * row_s) * col_s / denominator).astype(BF16)
    off_rows = pl.ds(off_at, off_piece)
    for k in plane:
        remote(stage.at[lax.div(k, W)], off_amp.at[off_rows],
               sems.at[10], sems.at[11], dev(z, k)).start()
    off_amp[off_rows, :] = stage[j]
    own_gathered.wait_send()
    off_lined.wait_send()
    send_b(1).wait_send()
    got_b(1).wait_recv()
    off_gathered = group(5, off_amp.at[pl.ds(0, (S - 1) * off_piece)])
    off_gathered.wait_send()
    off_gathered.wait_recv()


def finish(total_ref, other, off_amp, out_ref):
    j = lax.axis_index("pair")
    count = out_ref.shape[0]
    at = pl.ds(pl.multiple_of(pl.program_id(0) * count, count), count)

    @pl.when(j == 0)
    def _():
        out_ref[...] = (total_ref[at, :] + nt_dot(other[at, :], off_amp[...])).astype(BF16)

    @pl.when(j == 1)
    def _():
        out_ref[...] = (total_ref[at, :] + nn_dot(other[at, :], off_amp[...])).astype(BF16)


def pair_body(W, Z, three_index, occupied_energy, virtual_energy, tile_occupied, tile_virtual,
              tile_exponent):
    rows, width = three_index.shape
    S = 2 * W
    own_piece = width // W
    off_piece = width // S
    hbm = pl.BlockSpec(memory_space=pltpu.HBM)
    vmem = pl.BlockSpec(memory_space=pltpu.VMEM)
    dma = pltpu.SemaphoreType.DMA
    flops = 2 * rows * width * width
    total, other, off_amp = pl.pallas_call(
        functools.partial(kernel, W, Z),
        out_shape=[
            pltpu.VMEM((rows, width), F32),
            pltpu.VMEM((rows, width), BF16),
            pltpu.VMEM((width, width), BF16),
        ],
        in_specs=[hbm] * 6,
        out_specs=[vmem] * 3,
        scratch_shapes=[
            pltpu.VMEM((rows, width), BF16),
            pltpu.VMEM((VT, TS), F32),
            pltpu.SMEM(occupied_energy.shape, F32),
            pltpu.SMEM(tile_occupied.shape, jnp.int32),
            pltpu.SMEM(tile_virtual.shape, jnp.int32),
            pltpu.SMEM(tile_exponent.shape, jnp.int32),
            pltpu.VMEM((width, width), F32),
            pltpu.VMEM((width, width), F32),
            pltpu.VMEM((width, width), BF16),
            pltpu.VMEM((width, width), BF16),
            pltpu.VMEM((W, own_piece, width), BF16),
            pltpu.VMEM((S, off_piece, width), BF16),
            pltpu.VMEM((own_piece, width), BF16),
            pltpu.VMEM((off_piece, width), BF16),
            pltpu.VMEM((Z, own_piece, width), BF16),
            pltpu.VMEM((Z, off_piece, width), BF16),
            pltpu.VMEM((width, width), BF16),
            pltpu.VMEM((2, off_piece, width), BF16),
            pltpu.VMEM((8, TS), F32),
            dma((6,)),
            dma((2,)), dma((2,)),
            dma((12,)),
        ],
        compiler_params=pltpu.CompilerParams(
            collective_id=0, has_side_effects=True, vmem_limit_bytes=VMEM_LIMIT
        ),
        cost_estimate=pl.CostEstimate(
            flops=3 * flops, bytes_accessed=4 * rows * width, transcendentals=0
        ),
    )(three_index, virtual_energy.reshape(VT, TS), occupied_energy, tile_occupied, tile_virtual,
      tile_exponent)
    steps = 4
    return pl.pallas_call(
        finish,
        grid=(steps,),
        out_shape=jax.ShapeDtypeStruct((rows, width), BF16),
        in_specs=[vmem] * 3,
        out_specs=pl.BlockSpec((rows // steps, width), lambda i: (i, 0)),
        compiler_params=pltpu.CompilerParams(vmem_limit_bytes=8 * 1024 * 1024),
        cost_estimate=pl.CostEstimate(
            flops=flops, bytes_accessed=2 * rows * width, transcendentals=0
        ),
    )(total, other, off_amp)


def solution(mesh):
    placed = (P("aux", "pair"), P(), P(), P(), P(), P())
    W = 4
    Z = mesh.shape["aux"] // W

    def body(*args):
        if mesh.shape["pair"] == 2 and Z * W == 16 and args[0].shape[1] == 2 * TS:
            return pair_body(W, Z, *args)
        return general_body(*args)

    return jax.shard_map(
        body, mesh=mesh, in_specs=placed, out_specs=P("aux", "pair"), check_vma=False
    )
```

```python
import functools

import jax
import jax.numpy as jnp
from jax import lax
from jax.experimental import pallas as pl
from jax.experimental.pallas import tpu as pltpu
from jax.sharding import PartitionSpec as P

TS = 128
VT = 157
F32 = jnp.float32
BF16 = jnp.bfloat16
MESH = pl.DeviceIdType.MESH
VMEM_LIMIT = 60 * 1024 * 1024


def column_scale(tile_exponent):
    factor = jnp.where(tile_exponent == -1, 0.5, jnp.where(tile_exponent == 1, 2.0, 1.0)).astype(
        jnp.float32
    )
    return jnp.repeat(factor, TS)


def column_energy(occupied_energy, virtual_energy, tile_occupied, tile_virtual):
    virtual_cols = virtual_energy.reshape(VT, TS)[tile_virtual].reshape(-1)
    occupied_cols = jnp.repeat(occupied_energy[tile_occupied], TS)
    return virtual_cols - occupied_cols


def make_amplitude(coulomb, row_energy, row_scale, own_energy, own_scale):
    return (
        coulomb
        * (row_scale * row_scale)[:, None]
        * own_scale[None, :]
        / (row_energy[:, None] + own_energy[None, :])
    ).astype(jnp.bfloat16)


def general_body(
    three_index, occupied_energy, virtual_energy, tile_occupied, tile_virtual, tile_exponent
):
    width_local = three_index.shape[1]
    col_scale = column_scale(tile_exponent)
    col_energy = column_energy(occupied_energy, virtual_energy, tile_occupied, tile_virtual)
    offset = lax.axis_index("pair") * width_local
    own_energy = lax.dynamic_slice_in_dim(col_energy, offset, width_local)
    own_scale = lax.dynamic_slice_in_dim(col_scale, offset, width_local)
    contract = (((0,), (0,)), ((), ()))
    gathered = lax.all_gather(three_index, "pair", axis=1, tiled=True)
    coulomb = lax.dot_general(gathered, three_index, contract, preferred_element_type=jnp.float32)
    summed = lax.psum(coulomb, "aux")
    amplitude = make_amplitude(summed, col_energy, col_scale, own_energy, own_scale)
    result = jnp.dot(gathered, amplitude, preferred_element_type=jnp.float32)
    return result.astype(jnp.bfloat16)


def tn_dot(a, b):
    return lax.dot_general(a, b, (((0,), (0,)), ((), ())), preferred_element_type=F32)


def nt_dot(a, b):
    return lax.dot_general(a, b, (((1,), (1,)), ((), ())), preferred_element_type=F32)


def nn_dot(a, b):
    return jnp.dot(a, b, preferred_element_type=F32)


def kernel(
    W, Z, b_hbm, ve_hbm, occ_hbm, to_hbm, tv_hbm, te_hbm, out_ref,
    b_ref, ve_ref, occ_ref, to_ref, tv_ref, te_ref, own_product, other, off_amp,
    own_sum, off_sum, own_part, off_part, own_got, off_got, own_line, off_line,
    own_line_got, off_line_got, own_amp, stage, energy,
    load, b_s, b_r, sems,
):
    rows, width = b_ref.shape
    half = rows // 2
    S = 2 * W
    own_piece = width // W
    off_piece = width // S
    aux = lax.axis_index("aux")
    j = lax.axis_index("pair")
    z = lax.div(aux, W)
    w = lax.rem(aux, W)
    s = j * W + w

    def dev(line, place):
        return {"aux": line * W + lax.rem(place, W), "pair": lax.div(place, W)}

    def remote(src, dst, send, recv, target):
        return pltpu.make_async_remote_copy(
            src_ref=src, dst_ref=dst, send_sem=send, recv_sem=recv,
            device_id=target, device_id_type=MESH,
        )

    across = dev(z, lax.rem(s + W, S))
    plane = [lax.rem(s + i, S) for i in range(1, S)]
    side = [lax.rem(w + i, W) for i in range(1, W)]
    line = [lax.rem(z + i, Z) for i in range(1, Z)]

    loads = [
        pltpu.make_async_copy(src, dst, load.at[k])
        for k, (src, dst) in enumerate([
            (b_hbm, b_ref), (ve_hbm, ve_ref), (occ_hbm, occ_ref),
            (to_hbm, to_ref), (tv_hbm, tv_ref), (te_hbm, te_ref),
        ])
    ]
    barrier = pltpu.get_barrier_semaphore()
    for k in plane:
        pl.semaphore_signal(barrier, inc=1, device_id=dev(z, k), device_id_type=MESH)
    for k in line:
        pl.semaphore_signal(barrier, inc=1, device_id=dev(k, s), device_id_type=MESH)
    for one in loads:
        one.start()

    here = pl.multiple_of((1 - j) * half, half)
    away = pl.multiple_of(j * half, half)
    half_rows = [(away, here), (here, away)]
    own_at = pl.multiple_of(w * own_piece, own_piece)
    off_at = pl.multiple_of(s * off_piece, off_piece)

    def send_b(k):
        at = pl.ds(half_rows[k][0], half)
        return remote(b_hbm.at[at], other.at[at], b_s.at[k], b_r.at[k], across)

    def got_b(k):
        at = pl.ds(half_rows[k][1], half)
        return remote(b_hbm.at[at], other.at[at], b_s.at[k], b_r.at[k], across)

    def group(k, ref):
        return remote(ref, ref, sems.at[2 * k], sems.at[2 * k + 1], across)

    def scale(t):
        e = te_ref[t]
        return jnp.where(e == -1, 0.5, jnp.where(e == 1, 2.0, 1.0)).astype(F32)

    def down(row, first, count):
        shape = (count, TS)
        pick = lax.broadcasted_iota(jnp.int32, shape, 1) == (
            lax.broadcasted_iota(jnp.int32, shape, 0) + first)
        return jnp.sum(jnp.where(pick, row, 0.0), axis=1, keepdims=True)

    pl.semaphore_wait(barrier, S - 1 + Z - 1)
    send_b(0).start()

    loads[0].wait()
    own_sum[...] = tn_dot(b_ref[...], b_ref[...])
    own_part[...] = own_sum[...].astype(BF16)
    for k in side:
        remote(own_part.at[pl.ds(pl.multiple_of(k * own_piece, own_piece), own_piece)],
               own_got.at[w], sems.at[0], sems.at[1], dev(z, j * W + k)).start()

    for one in loads[1:]:
        one.wait()
    for t in range(4):
        energy[t:t + 1, :] = ve_ref[pl.ds(tv_ref[t], 1), :] - occ_ref[to_ref[t]]
    own_got[w] = jnp.zeros(own_got.shape[1:], BF16)
    off_got[s] = jnp.zeros(off_got.shape[1:], BF16)
    own_line_got[z] = jnp.zeros(own_line_got.shape[1:], BF16)
    off_line_got[z] = jnp.zeros(off_line_got.shape[1:], BF16)

    own_scattered = group(0, own_got.at[pl.ds(0, W - 1)])
    own_scattered.wait_recv()
    own_total = own_sum[pl.ds(own_at, own_piece), :]
    for k in range(W):
        own_total = own_total + own_got[k].astype(F32)
    own_line[...] = own_total.astype(BF16)
    for k in line:
        remote(own_line, own_line_got.at[z], sems.at[2], sems.at[3], dev(k, s)).start()

    here_rows = pl.ds(here, half)
    away_rows = pl.ds(away, half)
    send_b(0).wait_send()
    send_b(1).start()
    got_b(0).wait_recv()

    @pl.when(j == 0)
    def _():
        off_sum[...] = tn_dot(b_ref[here_rows, :], other[here_rows, :])

    @pl.when(j == 1)
    def _():
        off_sum[...] = tn_dot(other[here_rows, :], b_ref[here_rows, :])

    off_part[...] = off_sum[...].astype(BF16)
    for k in plane:
        remote(off_part.at[pl.ds(pl.multiple_of(k * off_piece, off_piece), off_piece)],
               off_got.at[s], sems.at[6], sems.at[7], dev(z, k)).start()

    own_lined = group(1, own_line_got.at[pl.ds(0, Z - 1)])
    own_lined.wait_recv()
    for k in range(Z):
        own_total = own_total + own_line_got[k].astype(F32)
    tile = lax.div(own_at, TS)
    row_e = down(energy[pl.ds(2 * j + tile, 1), :], lax.rem(own_at, TS), own_piece)
    row_s = scale(2 * j + tile)
    own_rows = pl.ds(own_at, own_piece)
    for h in range(2):
        cols = slice(h * TS, (h + 1) * TS)
        col_e = energy[pl.ds(2 * j + h, 1), :]
        col_s = scale(2 * j + h)
        own_amp[own_rows, cols] = (
            own_total[:, cols] * (row_s * row_s) * col_s / (row_e + col_e)
        ).astype(BF16)
    for k in side:
        remote(own_amp.at[own_rows], own_amp.at[own_rows],
               sems.at[4], sems.at[5], dev(z, j * W + k)).start()

    off_scattered = group(3, off_got.at[pl.ds(0, S - 1)])
    off_scattered.wait_recv()
    off_total = off_sum[pl.ds(off_at, off_piece), :]
    for k in range(S):
        off_total = off_total + off_got[k].astype(F32)
    off_line[...] = off_total.astype(BF16)
    for k in line:
        remote(off_line, off_line_got.at[z], sems.at[8], sems.at[9], dev(k, s)).start()

    own_gathered = group(2, own_amp.at[pl.ds(0, (W - 1) * own_piece)])
    own_gathered.wait_recv()
    own_product[...] = nn_dot(b_ref[...], own_amp[...])
    own_scattered.wait_send()
    own_lined.wait_send()
    off_scattered.wait_send()

    row_e = down(energy[pl.ds(j, 1), :], w * off_piece, off_piece)
    row_s = scale(j)
    off_lined = group(4, off_line_got.at[pl.ds(0, Z - 1)])
    off_lined.wait_recv()
    for k in range(Z):
        off_total = off_total + off_line_got[k].astype(F32)
    for h in range(2):
        cols = slice(h * TS, (h + 1) * TS)
        denominator = row_e + energy[2 + h:3 + h, :]
        col_s = scale(2 + h)
        value = off_total[:, cols]
        stage[0, :, cols] = (value * (col_s * col_s) * row_s / denominator).astype(BF16)
        stage[1, :, cols] = (value * (row_s * row_s) * col_s / denominator).astype(BF16)
    off_rows = pl.ds(off_at, off_piece)
    for k in plane:
        remote(stage.at[lax.div(k, W)], off_amp.at[off_rows],
               sems.at[10], sems.at[11], dev(z, k)).start()
    off_amp[off_rows, :] = stage[j]
    own_gathered.wait_send()
    off_lined.wait_send()
    off_gathered = group(5, off_amp.at[pl.ds(0, (S - 1) * off_piece)])
    off_gathered.wait_send()
    off_gathered.wait_recv()

    for at, later in ((here_rows, False), (away_rows, True)):
        if later:
            send_b(1).wait_send()
            got_b(1).wait_recv()

        @pl.when(j == 0)
        def _():
            out_ref[at, :] = (own_product[at, :] + nt_dot(other[at, :], off_amp[...])).astype(BF16)

        @pl.when(j == 1)
        def _():
            out_ref[at, :] = (own_product[at, :] + nn_dot(other[at, :], off_amp[...])).astype(BF16)


def pair_body(W, Z, three_index, occupied_energy, virtual_energy, tile_occupied, tile_virtual,
              tile_exponent):
    rows, width = three_index.shape
    S = 2 * W
    own_piece = width // W
    off_piece = width // S
    hbm = pl.BlockSpec(memory_space=pltpu.HBM)
    vmem = pl.BlockSpec(memory_space=pltpu.VMEM)
    dma = pltpu.SemaphoreType.DMA
    flops = 2 * rows * width * width
    return pl.pallas_call(
        functools.partial(kernel, W, Z),
        out_shape=pltpu.VMEM((rows, width), BF16),
        in_specs=[hbm] * 6,
        out_specs=vmem,
        scratch_shapes=[
            pltpu.VMEM((rows, width), BF16),
            pltpu.VMEM((VT, TS), F32),
            pltpu.SMEM(occupied_energy.shape, F32),
            pltpu.SMEM(tile_occupied.shape, jnp.int32),
            pltpu.SMEM(tile_virtual.shape, jnp.int32),
            pltpu.SMEM(tile_exponent.shape, jnp.int32),
            pltpu.VMEM((rows, width), F32),
            pltpu.VMEM((rows, width), BF16),
            pltpu.VMEM((width, width), BF16),
            pltpu.VMEM((width, width), F32),
            pltpu.VMEM((width, width), F32),
            pltpu.VMEM((width, width), BF16),
            pltpu.VMEM((width, width), BF16),
            pltpu.VMEM((W, own_piece, width), BF16),
            pltpu.VMEM((S, off_piece, width), BF16),
            pltpu.VMEM((own_piece, width), BF16),
            pltpu.VMEM((off_piece, width), BF16),
            pltpu.VMEM((Z, own_piece, width), BF16),
            pltpu.VMEM((Z, off_piece, width), BF16),
            pltpu.VMEM((width, width), BF16),
            pltpu.VMEM((2, off_piece, width), BF16),
            pltpu.VMEM((8, TS), F32),
            dma((6,)),
            dma((2,)), dma((2,)),
            dma((12,)),
        ],
        compiler_params=pltpu.CompilerParams(
            collective_id=0, has_side_effects=True, vmem_limit_bytes=VMEM_LIMIT
        ),
        cost_estimate=pl.CostEstimate(
            flops=4 * flops, bytes_accessed=4 * rows * width, transcendentals=0
        ),
    )(three_index, virtual_energy.reshape(VT, TS), occupied_energy, tile_occupied, tile_virtual,
      tile_exponent)


def solution(mesh):
    placed = (P("aux", "pair"), P(), P(), P(), P(), P())
    W = 4
    Z = mesh.shape["aux"] // W

    def body(*args):
        if mesh.shape["pair"] == 2 and Z * W == 16 and args[0].shape[1] == 2 * TS:
            return pair_body(W, Z, *args)
        return general_body(*args)

    return jax.shard_map(
        body, mesh=mesh, in_specs=placed, out_specs=P("aux", "pair"), check_vma=False
    )
```

```python
import functools

import jax
import jax.numpy as jnp
from jax import lax
from jax.experimental import pallas as pl
from jax.experimental.pallas import tpu as pltpu
from jax.sharding import PartitionSpec as P

TS = 128
VT = 157
F32 = jnp.float32
BF16 = jnp.bfloat16
MESH = pl.DeviceIdType.MESH
VMEM_LIMIT = 60 * 1024 * 1024


def column_scale(tile_exponent):
    factor = jnp.where(tile_exponent == -1, 0.5, jnp.where(tile_exponent == 1, 2.0, 1.0)).astype(
        jnp.float32
    )
    return jnp.repeat(factor, TS)


def column_energy(occupied_energy, virtual_energy, tile_occupied, tile_virtual):
    virtual_cols = virtual_energy.reshape(VT, TS)[tile_virtual].reshape(-1)
    occupied_cols = jnp.repeat(occupied_energy[tile_occupied], TS)
    return virtual_cols - occupied_cols


def make_amplitude(coulomb, row_energy, row_scale, own_energy, own_scale):
    return (
        coulomb
        * (row_scale * row_scale)[:, None]
        * own_scale[None, :]
        / (row_energy[:, None] + own_energy[None, :])
    ).astype(jnp.bfloat16)


def general_body(
    three_index, occupied_energy, virtual_energy, tile_occupied, tile_virtual, tile_exponent
):
    width_local = three_index.shape[1]
    col_scale = column_scale(tile_exponent)
    col_energy = column_energy(occupied_energy, virtual_energy, tile_occupied, tile_virtual)
    offset = lax.axis_index("pair") * width_local
    own_energy = lax.dynamic_slice_in_dim(col_energy, offset, width_local)
    own_scale = lax.dynamic_slice_in_dim(col_scale, offset, width_local)
    contract = (((0,), (0,)), ((), ()))
    gathered = lax.all_gather(three_index, "pair", axis=1, tiled=True)
    coulomb = lax.dot_general(gathered, three_index, contract, preferred_element_type=jnp.float32)
    summed = lax.psum(coulomb, "aux")
    amplitude = make_amplitude(summed, col_energy, col_scale, own_energy, own_scale)
    result = jnp.dot(gathered, amplitude, preferred_element_type=jnp.float32)
    return result.astype(jnp.bfloat16)


def tn_dot(a, b):
    return lax.dot_general(a, b, (((0,), (0,)), ((), ())), preferred_element_type=F32)


def nt_dot(a, b):
    return lax.dot_general(a, b, (((1,), (1,)), ((), ())), preferred_element_type=F32)


def nn_dot(a, b):
    return jnp.dot(a, b, preferred_element_type=F32)


def kernel(
    W, Z, parts, b_hbm, ve_hbm, occ_hbm, to_hbm, tv_hbm, te_hbm, out_ref,
    b_ref, ve_ref, occ_ref, to_ref, tv_ref, te_ref, own_product, other, off_amp,
    own_sum, off_sum, own_part, off_part, own_got, off_got, own_line, off_line,
    own_line_got, off_line_got, own_amp, stage, energy,
    load, b_s, b_r, sems,
):
    rows, width = b_ref.shape
    half = rows // 2
    S = 2 * W
    own_piece = width // W
    off_piece = width // S
    aux = lax.axis_index("aux")
    j = lax.axis_index("pair")
    z = lax.div(aux, W)
    w = lax.rem(aux, W)
    s = j * W + w

    def dev(line, place):
        return {"aux": line * W + lax.rem(place, W), "pair": lax.div(place, W)}

    def remote(src, dst, send, recv, target):
        return pltpu.make_async_remote_copy(
            src_ref=src, dst_ref=dst, send_sem=send, recv_sem=recv,
            device_id=target, device_id_type=MESH,
        )

    across = dev(z, lax.rem(s + W, S))
    plane = [lax.rem(s + i, S) for i in range(1, S)]
    side = [lax.rem(w + i, W) for i in range(1, W)]
    line = [lax.rem(z + i, Z) for i in range(1, Z)]

    loads = [
        pltpu.make_async_copy(src, dst, load.at[k])
        for k, (src, dst) in enumerate([
            (b_hbm, b_ref), (ve_hbm, ve_ref), (occ_hbm, occ_ref),
            (to_hbm, to_ref), (tv_hbm, tv_ref), (te_hbm, te_ref),
        ])
    ]
    barrier = pltpu.get_barrier_semaphore()
    for k in plane:
        pl.semaphore_signal(barrier, inc=1, device_id=dev(z, k), device_id_type=MESH)
    for k in line:
        pl.semaphore_signal(barrier, inc=1, device_id=dev(k, s), device_id_type=MESH)
    for one in loads:
        one.start()

    here = pl.multiple_of((1 - j) * half, half)
    away = pl.multiple_of(j * half, half)
    own_at = pl.multiple_of(w * own_piece, own_piece)
    off_at = pl.multiple_of(s * off_piece, off_piece)

    halves = [(away, here, parts[0]), (here, away, parts[1])]

    def b_copy(src, dst, k, p):
        sem = (len(parts[0]) if k else 0) + p
        return remote(b_hbm.at[src], other.at[dst], b_s.at[sem], b_r.at[sem], across)

    def b_rows(first, k, p):
        start, count = parts[k][p]
        return pl.ds(pl.multiple_of(first + start, 16), count)

    def send_b(k, p):
        at = b_rows(halves[k][0], k, p)
        return b_copy(at, at, k, p)

    def got_b(k, p):
        at = b_rows(halves[k][1], k, p)
        return b_copy(at, at, k, p)

    def group(k, ref):
        return remote(ref, ref, sems.at[2 * k], sems.at[2 * k + 1], across)

    def scale(t):
        e = te_ref[t]
        return jnp.where(e == -1, 0.5, jnp.where(e == 1, 2.0, 1.0)).astype(F32)

    def down(row, first, count):
        shape = (count, TS)
        pick = lax.broadcasted_iota(jnp.int32, shape, 1) == (
            lax.broadcasted_iota(jnp.int32, shape, 0) + first)
        return jnp.sum(jnp.where(pick, row, 0.0), axis=1, keepdims=True)

    pl.semaphore_wait(barrier, S - 1 + Z - 1)
    for p in range(len(parts[0])):
        send_b(0, p).start()

    loads[0].wait()
    own_sum[...] = tn_dot(b_ref[...], b_ref[...])
    own_part[...] = own_sum[...].astype(BF16)
    for k in side:
        remote(own_part.at[pl.ds(pl.multiple_of(k * own_piece, own_piece), own_piece)],
               own_got.at[w], sems.at[0], sems.at[1], dev(z, j * W + k)).start()

    for one in loads[1:]:
        one.wait()
    for t in range(4):
        energy[t:t + 1, :] = ve_ref[pl.ds(tv_ref[t], 1), :] - occ_ref[to_ref[t]]
    own_got[w] = jnp.zeros(own_got.shape[1:], BF16)
    off_got[s] = jnp.zeros(off_got.shape[1:], BF16)
    own_line_got[z] = jnp.zeros(own_line_got.shape[1:], BF16)
    off_line_got[z] = jnp.zeros(off_line_got.shape[1:], BF16)

    own_scattered = group(0, own_got.at[pl.ds(0, W - 1)])
    own_scattered.wait_recv()
    own_total = own_sum[pl.ds(own_at, own_piece), :]
    for k in range(W):
        own_total = own_total + own_got[k].astype(F32)
    own_line[...] = own_total.astype(BF16)
    for k in line:
        remote(own_line, own_line_got.at[z], sems.at[2], sems.at[3], dev(k, s)).start()

    for p in range(len(parts[0])):
        if p == len(parts[0]) - 1:
            for sent in range(len(parts[0])):
                send_b(0, sent).wait_send()
            send_b(1, 0).start()
        got_b(0, p).wait_recv()
        at = b_rows(here, 0, p)

        @pl.when(j == 0)
        def _():
            value = tn_dot(b_ref[at, :], other[at, :])
            off_sum[...] = value if p == 0 else off_sum[...] + value

        @pl.when(j == 1)
        def _():
            value = tn_dot(other[at, :], b_ref[at, :])
            off_sum[...] = value if p == 0 else off_sum[...] + value

    off_part[...] = off_sum[...].astype(BF16)
    for k in plane:
        remote(off_part.at[pl.ds(pl.multiple_of(k * off_piece, off_piece), off_piece)],
               off_got.at[s], sems.at[6], sems.at[7], dev(z, k)).start()

    off_scattered = group(3, off_got.at[pl.ds(0, S - 1)])
    off_scattered.wait_recv()
    send_b(1, 1).start()
    off_total = off_sum[pl.ds(off_at, off_piece), :]
    for k in range(S):
        off_total = off_total + off_got[k].astype(F32)
    off_line[...] = off_total.astype(BF16)
    for k in line:
        remote(off_line, off_line_got.at[z], sems.at[8], sems.at[9], dev(k, s)).start()

    own_lined = group(1, own_line_got.at[pl.ds(0, Z - 1)])
    own_lined.wait_recv()
    for k in range(Z):
        own_total = own_total + own_line_got[k].astype(F32)
    tile = lax.div(own_at, TS)
    row_e = down(energy[pl.ds(2 * j + tile, 1), :], lax.rem(own_at, TS), own_piece)
    row_s = scale(2 * j + tile)
    own_rows = pl.ds(own_at, own_piece)
    for h in range(2):
        cols = slice(h * TS, (h + 1) * TS)
        col_e = energy[pl.ds(2 * j + h, 1), :]
        col_s = scale(2 * j + h)
        own_amp[own_rows, cols] = (
            own_total[:, cols] * (row_s * row_s) * col_s / (row_e + col_e)
        ).astype(BF16)
    for k in side:
        remote(own_amp.at[own_rows], own_amp.at[own_rows],
               sems.at[4], sems.at[5], dev(z, j * W + k)).start()
    own_scattered.wait_send()
    own_lined.wait_send()
    off_scattered.wait_send()

    row_e = down(energy[pl.ds(j, 1), :], w * off_piece, off_piece)
    row_s = scale(j)
    off_lined = group(4, off_line_got.at[pl.ds(0, Z - 1)])
    off_lined.wait_recv()
    for k in range(Z):
        off_total = off_total + off_line_got[k].astype(F32)
    for h in range(2):
        cols = slice(h * TS, (h + 1) * TS)
        denominator = row_e + energy[2 + h:3 + h, :]
        col_s = scale(2 + h)
        value = off_total[:, cols]
        stage[0, :, cols] = (value * (col_s * col_s) * row_s / denominator).astype(BF16)
        stage[1, :, cols] = (value * (row_s * row_s) * col_s / denominator).astype(BF16)
    off_rows = pl.ds(off_at, off_piece)
    for k in plane:
        remote(stage.at[lax.div(k, W)], off_amp.at[off_rows],
               sems.at[10], sems.at[11], dev(z, k)).start()
    send_b(1, 2).start()
    off_amp[off_rows, :] = stage[j]

    own_gathered = group(2, own_amp.at[pl.ds(0, (W - 1) * own_piece)])
    own_gathered.wait_recv()
    own_product[...] = nn_dot(b_ref[...], own_amp[...])
    own_gathered.wait_send()
    off_lined.wait_send()
    off_gathered = group(5, off_amp.at[pl.ds(0, (S - 1) * off_piece)])
    off_gathered.wait_send()
    send_b(1, 0).wait_send()
    send_b(1, 1).wait_send()
    off_gathered.wait_recv()

    def result(at):
        @pl.when(j == 0)
        def _():
            out_ref[at, :] = (own_product[at, :] + nt_dot(other[at, :], off_amp[...])).astype(BF16)

        @pl.when(j == 1)
        def _():
            out_ref[at, :] = (own_product[at, :] + nn_dot(other[at, :], off_amp[...])).astype(BF16)

    result(pl.ds(here, half))
    for p in range(3):
        got_b(1, p).wait_recv()
        if p > 0:
            start, count = parts[1][p]
            if p == 1:
                start, count = 0, parts[1][0][1] + count
            result(pl.ds(pl.multiple_of(away + start, 16), count))
    send_b(1, 2).wait_send()


def pair_body(W, Z, three_index, occupied_energy, virtual_energy, tile_occupied, tile_virtual,
              tile_exponent):
    rows, width = three_index.shape
    S = 2 * W
    own_piece = width // W
    off_piece = width // S
    half = rows // 2
    first = half // 32 * 16
    small = half // 112 * 16
    parts = (
        ((0, first), (first, half - first)),
        ((0, small), (small, first), (small + first, half - first - small)),
    )
    hbm = pl.BlockSpec(memory_space=pltpu.HBM)
    vmem = pl.BlockSpec(memory_space=pltpu.VMEM)
    dma = pltpu.SemaphoreType.DMA
    flops = 2 * rows * width * width
    return pl.pallas_call(
        functools.partial(kernel, W, Z, parts),
        out_shape=pltpu.VMEM((rows, width), BF16),
        in_specs=[hbm] * 6,
        out_specs=vmem,
        scratch_shapes=[
            pltpu.VMEM((rows, width), BF16),
            pltpu.VMEM((VT, TS), F32),
            pltpu.SMEM(occupied_energy.shape, F32),
            pltpu.SMEM(tile_occupied.shape, jnp.int32),
            pltpu.SMEM(tile_virtual.shape, jnp.int32),
            pltpu.SMEM(tile_exponent.shape, jnp.int32),
            pltpu.VMEM((rows, width), F32),
            pltpu.VMEM((rows, width), BF16),
            pltpu.VMEM((width, width), BF16),
            pltpu.VMEM((width, width), F32),
            pltpu.VMEM((width, width), F32),
            pltpu.VMEM((width, width), BF16),
            pltpu.VMEM((width, width), BF16),
            pltpu.VMEM((W, own_piece, width), BF16),
            pltpu.VMEM((S, off_piece, width), BF16),
            pltpu.VMEM((own_piece, width), BF16),
            pltpu.VMEM((off_piece, width), BF16),
            pltpu.VMEM((Z, own_piece, width), BF16),
            pltpu.VMEM((Z, off_piece, width), BF16),
            pltpu.VMEM((width, width), BF16),
            pltpu.VMEM((2, off_piece, width), BF16),
            pltpu.VMEM((8, TS), F32),
            dma((6,)),
            dma((5,)), dma((5,)),
            dma((12,)),
        ],
        compiler_params=pltpu.CompilerParams(
            collective_id=0, has_side_effects=True, vmem_limit_bytes=VMEM_LIMIT
        ),
        cost_estimate=pl.CostEstimate(
            flops=4 * flops, bytes_accessed=4 * rows * width, transcendentals=0
        ),
    )(three_index, virtual_energy.reshape(VT, TS), occupied_energy, tile_occupied, tile_virtual,
      tile_exponent)


def solution(mesh):
    placed = (P("aux", "pair"), P(), P(), P(), P(), P())
    W = 4
    Z = mesh.shape["aux"] // W

    def body(*args):
        if mesh.shape["pair"] == 2 and Z * W == 16 and args[0].shape[1] == 2 * TS and args[0].shape[0] % 224 == 0:
            return pair_body(W, Z, *args)
        return general_body(*args)

    return jax.shard_map(
        body, mesh=mesh, in_specs=placed, out_specs=P("aux", "pair"), check_vma=False
    )
```

```python
import functools

import jax
import jax.numpy as jnp
from jax import lax
from jax.experimental import pallas as pl
from jax.experimental.pallas import tpu as pltpu
from jax.sharding import PartitionSpec as P

TS = 128
VT = 157
F32 = jnp.float32
BF16 = jnp.bfloat16
MESH = pl.DeviceIdType.MESH
VMEM_LIMIT = 60 * 1024 * 1024


def column_scale(tile_exponent):
    factor = jnp.where(tile_exponent == -1, 0.5, jnp.where(tile_exponent == 1, 2.0, 1.0)).astype(
        jnp.float32
    )
    return jnp.repeat(factor, TS)


def column_energy(occupied_energy, virtual_energy, tile_occupied, tile_virtual):
    virtual_cols = virtual_energy.reshape(VT, TS)[tile_virtual].reshape(-1)
    occupied_cols = jnp.repeat(occupied_energy[tile_occupied], TS)
    return virtual_cols - occupied_cols


def make_amplitude(coulomb, row_energy, row_scale, own_energy, own_scale):
    return (
        coulomb
        * (row_scale * row_scale)[:, None]
        * own_scale[None, :]
        / (row_energy[:, None] + own_energy[None, :])
    ).astype(jnp.bfloat16)


def general_body(
    three_index, occupied_energy, virtual_energy, tile_occupied, tile_virtual, tile_exponent
):
    width_local = three_index.shape[1]
    col_scale = column_scale(tile_exponent)
    col_energy = column_energy(occupied_energy, virtual_energy, tile_occupied, tile_virtual)
    offset = lax.axis_index("pair") * width_local
    own_energy = lax.dynamic_slice_in_dim(col_energy, offset, width_local)
    own_scale = lax.dynamic_slice_in_dim(col_scale, offset, width_local)
    contract = (((0,), (0,)), ((), ()))
    gathered = lax.all_gather(three_index, "pair", axis=1, tiled=True)
    coulomb = lax.dot_general(gathered, three_index, contract, preferred_element_type=jnp.float32)
    summed = lax.psum(coulomb, "aux")
    amplitude = make_amplitude(summed, col_energy, col_scale, own_energy, own_scale)
    result = jnp.dot(gathered, amplitude, preferred_element_type=jnp.float32)
    return result.astype(jnp.bfloat16)


def tn_dot(a, b):
    return lax.dot_general(a, b, (((0,), (0,)), ((), ())), preferred_element_type=F32)


def nt_dot(a, b):
    return lax.dot_general(a, b, (((1,), (1,)), ((), ())), preferred_element_type=F32)


def nn_dot(a, b):
    return jnp.dot(a, b, preferred_element_type=F32)


def kernel(
    W, Z, parts, b_hbm, ve_hbm, occ_hbm, to_hbm, tv_hbm, te_hbm, out_ref,
    b_ref, ve_ref, occ_ref, to_ref, tv_ref, te_ref, own_product, other, off_amp,
    own_sum, off_send, off_core, off_sum, own_part, off_part, own_got, off_got, own_line, off_line,
    own_line_got, off_line_got, own_amp, stage, energy,
    load, b_s, b_r, core_s, core_r, sems,
):
    rows, width = b_ref.shape
    half = rows // 2
    S = 2 * W
    U = W
    own_piece = width // W
    off_piece = width // S
    aux = lax.axis_index("aux")
    j = lax.axis_index("pair")
    z = lax.div(aux, W)
    w = lax.rem(aux, W)
    s = j * W + w
    core = lax.rem(w, 2)
    u = lax.div(s, 2)

    def dev(line, place):
        return {"aux": line * W + lax.rem(place, W), "pair": lax.div(place, W)}

    def remote(src, dst, send, recv, target):
        return pltpu.make_async_remote_copy(
            src_ref=src, dst_ref=dst, send_sem=send, recv_sem=recv,
            device_id=target, device_id_type=MESH,
        )

    across = dev(z, lax.rem(s + W, S))
    sibling = dev(z, 2 * u + 1 - core)
    equal = [lax.rem(u + i, U) for i in range(1, U)]
    side = [lax.rem(w + i, W) for i in range(1, W)]
    line = [lax.rem(z + i, Z) for i in range(1, Z)]

    loads = [
        pltpu.make_async_copy(src, dst, load.at[k])
        for k, (src, dst) in enumerate([
            (b_hbm, b_ref), (ve_hbm, ve_ref), (occ_hbm, occ_ref),
            (to_hbm, to_ref), (tv_hbm, tv_ref), (te_hbm, te_ref),
        ])
    ]
    barrier = pltpu.get_barrier_semaphore()
    greeted = [dev(z, j * W + k) for k in side]
    greeted += [dev(z, lax.rem((1 - j) * W + 2 * i + core, S)) for i in range(W // 2)]
    for target in greeted:
        pl.semaphore_signal(barrier, inc=1, device_id=target, device_id_type=MESH)
    for k in line:
        pl.semaphore_signal(barrier, inc=1, device_id=dev(k, s), device_id_type=MESH)
    for one in loads:
        one.start()

    here = pl.multiple_of((1 - j) * half, half)
    away = pl.multiple_of(j * half, half)
    own_at = pl.multiple_of(w * own_piece, own_piece)
    mine = pl.multiple_of(core * TS, TS)
    theirs = pl.multiple_of((1 - core) * TS, TS)
    off_at = pl.multiple_of(u * off_piece, off_piece)
    off_rows = pl.ds(pl.multiple_of(core * TS + u * off_piece, off_piece), off_piece)

    halves = [(away, here, parts[0]), (here, away, parts[1])]

    def b_copy(src, dst, k, p):
        sem = (len(parts[0]) if k else 0) + p
        return remote(b_hbm.at[src], other.at[dst], b_s.at[sem], b_r.at[sem], across)

    def b_rows(first, k, p):
        start, count = parts[k][p]
        return pl.ds(pl.multiple_of(first + start, 16), count)

    def send_b(k, p):
        at = b_rows(halves[k][0], k, p)
        return b_copy(at, at, k, p)

    def got_b(k, p):
        at = b_rows(halves[k][1], k, p)
        return b_copy(at, at, k, p)

    def group(k, ref):
        return remote(ref, ref, sems.at[2 * k], sems.at[2 * k + 1], across)

    def scale(t):
        e = te_ref[t]
        return jnp.where(e == -1, 0.5, jnp.where(e == 1, 2.0, 1.0)).astype(F32)

    def down(row, first, count):
        shape = (count, TS)
        pick = lax.broadcasted_iota(jnp.int32, shape, 1) == (
            lax.broadcasted_iota(jnp.int32, shape, 0) + first)
        return jnp.sum(jnp.where(pick, row, 0.0), axis=1, keepdims=True)

    pl.semaphore_wait(barrier, len(greeted) + Z - 1)
    for p in range(len(parts[0])):
        send_b(0, p).start()

    loads[0].wait()
    own_sum[...] = tn_dot(b_ref[...], b_ref[...])
    own_part[...] = own_sum[...].astype(BF16)
    for k in side:
        remote(own_part.at[pl.ds(pl.multiple_of(k * own_piece, own_piece), own_piece)],
               own_got.at[w], sems.at[0], sems.at[1], dev(z, j * W + k)).start()

    for one in loads[1:]:
        one.wait()
    for t in range(4):
        energy[t:t + 1, :] = ve_ref[pl.ds(tv_ref[t], 1), :] - occ_ref[to_ref[t]]
    own_got[w] = jnp.zeros(own_got.shape[1:], BF16)
    off_got[u] = jnp.zeros(off_got.shape[1:], BF16)
    own_line_got[z] = jnp.zeros(own_line_got.shape[1:], BF16)
    off_line_got[z] = jnp.zeros(off_line_got.shape[1:], BF16)

    own_scattered = group(0, own_got.at[pl.ds(0, W - 1)])
    own_scattered.wait_recv()
    own_total = own_sum[pl.ds(own_at, own_piece), :]
    for k in range(W):
        own_total = own_total + own_got[k].astype(F32)
    own_line[...] = own_total.astype(BF16)
    for k in line:
        remote(own_line, own_line_got.at[z], sems.at[2], sems.at[3], dev(k, s)).start()

    off_core_copy = remote(off_send, off_core, core_s.at[0], core_r.at[0], sibling)
    for p in range(len(parts[0])):
        if p == len(parts[0]) - 1:
            for sent in range(len(parts[0])):
                send_b(0, sent).wait_send()
            send_b(1, 0).start()
        got_b(0, p).wait_recv()
        at = b_rows(here, 0, p)

        def product(target, cols):
            @pl.when(j == 0)
            def _():
                value = tn_dot(b_ref[at, pl.ds(cols, TS)], other[at, :])
                target[...] = value if p == 0 else target[...] + value

            @pl.when(j == 1)
            def _():
                value = tn_dot(other[at, pl.ds(cols, TS)], b_ref[at, :])
                target[...] = value if p == 0 else target[...] + value

        product(off_send, theirs)
        if p == len(parts[0]) - 1:
            off_core_copy.start()
        product(off_sum, mine)

    off_core_copy.wait_recv()
    off_sum[...] += off_core[...]
    off_part[...] = off_sum[...].astype(BF16)
    for k in equal:
        remote(off_part.at[pl.ds(pl.multiple_of(k * off_piece, off_piece), off_piece)],
               off_got.at[u], sems.at[6], sems.at[7], dev(z, 2 * k + core)).start()

    off_scattered = group(3, off_got.at[pl.ds(0, U - 1)])
    off_scattered.wait_send()
    send_b(1, 1).start()
    off_scattered.wait_recv()
    off_total = off_sum[pl.ds(off_at, off_piece), :]
    for k in range(U):
        off_total = off_total + off_got[k].astype(F32)
    off_line[...] = off_total.astype(BF16)
    for k in line:
        remote(off_line, off_line_got.at[z], sems.at[8], sems.at[9], dev(k, s)).start()

    own_lined = group(1, own_line_got.at[pl.ds(0, Z - 1)])
    own_lined.wait_recv()
    for k in range(Z):
        own_total = own_total + own_line_got[k].astype(F32)
    tile = lax.div(own_at, TS)
    row_e = down(energy[pl.ds(2 * j + tile, 1), :], lax.rem(own_at, TS), own_piece)
    row_s = scale(2 * j + tile)
    own_rows = pl.ds(own_at, own_piece)
    for h in range(2):
        cols = slice(h * TS, (h + 1) * TS)
        col_e = energy[pl.ds(2 * j + h, 1), :]
        col_s = scale(2 * j + h)
        own_amp[own_rows, cols] = (
            own_total[:, cols] * (row_s * row_s) * col_s / (row_e + col_e)
        ).astype(BF16)
    for k in side:
        remote(own_amp.at[own_rows], own_amp.at[own_rows],
               sems.at[4], sems.at[5], dev(z, j * W + k)).start()
    own_scattered.wait_send()
    own_lined.wait_send()
    off_core_copy.wait_send()

    row_e = down(energy[pl.ds(core, 1), :], u * off_piece, off_piece)
    row_s = scale(core)
    off_lined = group(4, off_line_got.at[pl.ds(0, Z - 1)])
    off_lined.wait_recv()
    for k in range(Z):
        off_total = off_total + off_line_got[k].astype(F32)
    for h in range(2):
        cols = slice(h * TS, (h + 1) * TS)
        denominator = row_e + energy[2 + h:3 + h, :]
        col_s = scale(2 + h)
        value = off_total[:, cols]
        stage[0, :, cols] = (value * (col_s * col_s) * row_s / denominator).astype(BF16)
        stage[1, :, cols] = (value * (row_s * row_s) * col_s / denominator).astype(BF16)
    for k in equal:
        remote(stage.at[lax.div(k, U // 2)], off_amp.at[off_rows],
               sems.at[10], sems.at[11], dev(z, 2 * k + core)).start()
    off_amp[off_rows, :] = stage[j]
    off_gathered = group(5, off_amp.at[pl.ds(0, (U - 1) * off_piece)])
    off_gathered.wait_send()
    send_b(1, 2).start()

    own_gathered = group(2, own_amp.at[pl.ds(0, (W - 1) * own_piece)])
    own_gathered.wait_recv()
    own_product[...] = nn_dot(b_ref[...], own_amp[...])
    off_gathered.wait_recv()

    def forward(first):
        place = off_amp.at[pl.ds(first, TS)]
        return remote(place, place, core_s.at[1], core_r.at[1], sibling)

    forward(mine).start()
    own_gathered.wait_send()
    off_lined.wait_send()
    send_b(1, 0).wait_send()
    send_b(1, 1).wait_send()
    forward(theirs).wait_recv()

    def result(at):
        @pl.when(j == 0)
        def _():
            out_ref[at, :] = (own_product[at, :] + nt_dot(other[at, :], off_amp[...])).astype(BF16)

        @pl.when(j == 1)
        def _():
            out_ref[at, :] = (own_product[at, :] + nn_dot(other[at, :], off_amp[...])).astype(BF16)

    result(pl.ds(here, half))
    for p in range(3):
        got_b(1, p).wait_recv()
        if p > 0:
            start, count = parts[1][p]
            if p == 1:
                start, count = 0, parts[1][0][1] + count
            result(pl.ds(pl.multiple_of(away + start, 16), count))
    send_b(1, 2).wait_send()
    forward(mine).wait_send()


def pair_body(W, Z, three_index, occupied_energy, virtual_energy, tile_occupied, tile_virtual,
              tile_exponent):
    rows, width = three_index.shape
    S = 2 * W
    own_piece = width // W
    off_piece = width // S
    half = rows // 2
    first = half // 32 * 16
    small = 2 * half // 112 * 16
    middle = half // 32 * 16 - 16
    parts = (
        ((0, first), (first, half - first)),
        ((0, small), (small, middle), (small + middle, half - middle - small)),
    )
    hbm = pl.BlockSpec(memory_space=pltpu.HBM)
    vmem = pl.BlockSpec(memory_space=pltpu.VMEM)
    dma = pltpu.SemaphoreType.DMA
    flops = 2 * rows * width * width
    return pl.pallas_call(
        functools.partial(kernel, W, Z, parts),
        out_shape=pltpu.VMEM((rows, width), BF16),
        in_specs=[hbm] * 6,
        out_specs=vmem,
        scratch_shapes=[
            pltpu.VMEM((rows, width), BF16),
            pltpu.VMEM((VT, TS), F32),
            pltpu.SMEM(occupied_energy.shape, F32),
            pltpu.SMEM(tile_occupied.shape, jnp.int32),
            pltpu.SMEM(tile_virtual.shape, jnp.int32),
            pltpu.SMEM(tile_exponent.shape, jnp.int32),
            pltpu.VMEM((rows, width), F32),
            pltpu.VMEM((rows, width), BF16),
            pltpu.VMEM((width, width), BF16),
            pltpu.VMEM((width, width), F32),
            pltpu.VMEM((TS, width), F32),
            pltpu.VMEM((TS, width), F32),
            pltpu.VMEM((TS, width), F32),
            pltpu.VMEM((width, width), BF16),
            pltpu.VMEM((TS, width), BF16),
            pltpu.VMEM((W, own_piece, width), BF16),
            pltpu.VMEM((W, off_piece, width), BF16),
            pltpu.VMEM((own_piece, width), BF16),
            pltpu.VMEM((off_piece, width), BF16),
            pltpu.VMEM((Z, own_piece, width), BF16),
            pltpu.VMEM((Z, off_piece, width), BF16),
            pltpu.VMEM((width, width), BF16),
            pltpu.VMEM((2, off_piece, width), BF16),
            pltpu.VMEM((8, TS), F32),
            dma((6,)),
            dma((5,)), dma((5,)),
            dma((2,)), dma((2,)),
            dma((12,)),
        ],
        compiler_params=pltpu.CompilerParams(
            collective_id=0, has_side_effects=True, vmem_limit_bytes=VMEM_LIMIT
        ),
        cost_estimate=pl.CostEstimate(
            flops=4 * flops, bytes_accessed=4 * rows * width, transcendentals=0
        ),
    )(three_index, virtual_energy.reshape(VT, TS), occupied_energy, tile_occupied, tile_virtual,
      tile_exponent)


def solution(mesh):
    placed = (P("aux", "pair"), P(), P(), P(), P(), P())
    W = 4
    Z = mesh.shape["aux"] // W

    def body(*args):
        if mesh.shape["pair"] == 2 and Z * W == 16 and args[0].shape[1] == 2 * TS and args[0].shape[0] % 224 == 0:
            return pair_body(W, Z, *args)
        return general_body(*args)

    return jax.shard_map(
        body, mesh=mesh, in_specs=placed, out_specs=P("aux", "pair"), check_vma=False
    )
```

```python
import functools

import jax
import jax.numpy as jnp
from jax import lax
from jax.experimental import pallas as pl
from jax.experimental.pallas import tpu as pltpu
from jax.sharding import PartitionSpec as P

TS = 128
VT = 157
F32 = jnp.float32
BF16 = jnp.bfloat16
MESH = pl.DeviceIdType.MESH
VMEM_LIMIT = 60 * 1024 * 1024


def column_scale(tile_exponent):
    factor = jnp.where(tile_exponent == -1, 0.5, jnp.where(tile_exponent == 1, 2.0, 1.0)).astype(
        jnp.float32
    )
    return jnp.repeat(factor, TS)


def column_energy(occupied_energy, virtual_energy, tile_occupied, tile_virtual):
    virtual_cols = virtual_energy.reshape(VT, TS)[tile_virtual].reshape(-1)
    occupied_cols = jnp.repeat(occupied_energy[tile_occupied], TS)
    return virtual_cols - occupied_cols


def make_amplitude(coulomb, row_energy, row_scale, own_energy, own_scale):
    return (
        coulomb
        * (row_scale * row_scale)[:, None]
        * own_scale[None, :]
        / (row_energy[:, None] + own_energy[None, :])
    ).astype(jnp.bfloat16)


def general_body(
    three_index, occupied_energy, virtual_energy, tile_occupied, tile_virtual, tile_exponent
):
    width_local = three_index.shape[1]
    col_scale = column_scale(tile_exponent)
    col_energy = column_energy(occupied_energy, virtual_energy, tile_occupied, tile_virtual)
    offset = lax.axis_index("pair") * width_local
    own_energy = lax.dynamic_slice_in_dim(col_energy, offset, width_local)
    own_scale = lax.dynamic_slice_in_dim(col_scale, offset, width_local)
    contract = (((0,), (0,)), ((), ()))
    gathered = lax.all_gather(three_index, "pair", axis=1, tiled=True)
    coulomb = lax.dot_general(gathered, three_index, contract, preferred_element_type=jnp.float32)
    summed = lax.psum(coulomb, "aux")
    amplitude = make_amplitude(summed, col_energy, col_scale, own_energy, own_scale)
    result = jnp.dot(gathered, amplitude, preferred_element_type=jnp.float32)
    return result.astype(jnp.bfloat16)


def tn_dot(a, b):
    return lax.dot_general(a, b, (((0,), (0,)), ((), ())), preferred_element_type=F32)


def nt_dot(a, b):
    return lax.dot_general(a, b, (((1,), (1,)), ((), ())), preferred_element_type=F32)


def nn_dot(a, b):
    return jnp.dot(a, b, preferred_element_type=F32)


def kernel(
    W, Z, parts, b_hbm, ve_hbm, occ_hbm, to_hbm, tv_hbm, te_hbm, out_ref,
    b_ref, ve_ref, occ_ref, to_ref, tv_ref, te_ref, own_product, other, off_amp,
    own_sum, off_sum, own_part, off_part, own_got, off_got, own_line, off_line,
    own_line_got, off_line_got, own_amp, stage, energy,
    load, b_s, b_r, sems,
):
    rows, width = b_ref.shape
    half = rows // 2
    S = 2 * W
    own_piece = width // W
    off_piece = width // S
    aux = lax.axis_index("aux")
    j = lax.axis_index("pair")
    z = lax.div(aux, W)
    w = lax.rem(aux, W)
    s = j * W + w

    def dev(line, place):
        return {"aux": line * W + lax.rem(place, W), "pair": lax.div(place, W)}

    def remote(src, dst, send, recv, target):
        return pltpu.make_async_remote_copy(
            src_ref=src, dst_ref=dst, send_sem=send, recv_sem=recv,
            device_id=target, device_id_type=MESH,
        )

    across = dev(z, lax.rem(s + W, S))
    plane = [lax.rem(s + i, S) for i in range(1, S)]
    side = [lax.rem(w + i, W) for i in range(1, W)]
    line = [lax.rem(z + i, Z) for i in range(1, Z)]

    loads = [
        pltpu.make_async_copy(src, dst, load.at[k])
        for k, (src, dst) in enumerate([
            (b_hbm, b_ref), (ve_hbm, ve_ref), (occ_hbm, occ_ref),
            (to_hbm, to_ref), (tv_hbm, tv_ref), (te_hbm, te_ref),
        ])
    ]
    barrier = pltpu.get_barrier_semaphore()
    for k in plane:
        pl.semaphore_signal(barrier, inc=1, device_id=dev(z, k), device_id_type=MESH)
    for k in line:
        pl.semaphore_signal(barrier, inc=1, device_id=dev(k, s), device_id_type=MESH)
    for one in loads:
        one.start()

    here = pl.multiple_of((1 - j) * half, half)
    away = pl.multiple_of(j * half, half)
    own_at = pl.multiple_of(w * own_piece, own_piece)
    off_at = pl.multiple_of(s * off_piece, off_piece)

    halves = [(away, here, parts[0]), (here, away, parts[1])]

    def b_copy(src, dst, k, p):
        sem = (len(parts[0]) if k else 0) + p
        return remote(b_ref.at[src], other.at[dst], b_s.at[sem], b_r.at[sem], across)

    def b_rows(first, k, p):
        start, count = parts[k][p]
        return pl.ds(pl.multiple_of(first + start, 16), count)

    def send_b(k, p):
        at = b_rows(halves[k][0], k, p)
        return b_copy(at, at, k, p)

    def got_b(k, p):
        at = b_rows(halves[k][1], k, p)
        return b_copy(at, at, k, p)

    def group(k, ref):
        return remote(ref, ref, sems.at[2 * k], sems.at[2 * k + 1], across)

    def scale(t):
        e = te_ref[t]
        return jnp.where(e == -1, 0.5, jnp.where(e == 1, 2.0, 1.0)).astype(F32)

    def down(row, first, count):
        shape = (count, TS)
        pick = lax.broadcasted_iota(jnp.int32, shape, 1) == (
            lax.broadcasted_iota(jnp.int32, shape, 0) + first)
        return jnp.sum(jnp.where(pick, row, 0.0), axis=1, keepdims=True)

    pl.semaphore_wait(barrier, S - 1 + Z - 1)
    loads[0].wait()
    for p in range(len(parts[0])):
        send_b(0, p).start()

    own_sum[...] = tn_dot(b_ref[...], b_ref[...])
    own_part[...] = own_sum[...].astype(BF16)
    for k in side:
        remote(own_part.at[pl.ds(pl.multiple_of(k * own_piece, own_piece), own_piece)],
               own_got.at[w], sems.at[0], sems.at[1], dev(z, j * W + k)).start()

    for one in loads[1:]:
        one.wait()
    for t in range(4):
        energy[t:t + 1, :] = ve_ref[pl.ds(tv_ref[t], 1), :] - occ_ref[to_ref[t]]
    own_got[w] = jnp.zeros(own_got.shape[1:], BF16)
    off_got[s] = jnp.zeros(off_got.shape[1:], BF16)
    own_line_got[z] = jnp.zeros(own_line_got.shape[1:], BF16)
    off_line_got[z] = jnp.zeros(off_line_got.shape[1:], BF16)

    own_scattered = group(0, own_got.at[pl.ds(0, W - 1)])
    own_scattered.wait_recv()
    own_total = own_sum[pl.ds(own_at, own_piece), :]
    for k in range(W):
        own_total = own_total + own_got[k].astype(F32)
    own_line[...] = own_total.astype(BF16)
    for k in line:
        remote(own_line, own_line_got.at[z], sems.at[2], sems.at[3], dev(k, s)).start()

    for p in range(0, len(parts[0]), 2):
        if p == len(parts[0]) - 2:
            for sent in range(len(parts[0])):
                send_b(0, sent).wait_send()
            send_b(1, 0).start()
        got_b(0, p).wait_recv()
        got_b(0, p + 1).wait_recv()
        at = pl.ds(pl.multiple_of(here + parts[0][p][0], 16), parts[0][p][1] + parts[0][p + 1][1])

        @pl.when(j == 0)
        def _():
            value = tn_dot(b_ref[at, :], other[at, :])
            off_sum[...] = value if p == 0 else off_sum[...] + value

        @pl.when(j == 1)
        def _():
            value = tn_dot(other[at, :], b_ref[at, :])
            off_sum[...] = value if p == 0 else off_sum[...] + value

    off_part[...] = off_sum[...].astype(BF16)
    for k in plane:
        remote(off_part.at[pl.ds(pl.multiple_of(k * off_piece, off_piece), off_piece)],
               off_got.at[s], sems.at[6], sems.at[7], dev(z, k)).start()

    off_scattered = group(3, off_got.at[pl.ds(0, S - 1)])
    off_scattered.wait_recv()
    send_b(1, 1).start()
    off_total = off_sum[pl.ds(off_at, off_piece), :]
    for k in range(S):
        off_total = off_total + off_got[k].astype(F32)
    off_line[...] = off_total.astype(BF16)
    for k in line:
        remote(off_line, off_line_got.at[z], sems.at[8], sems.at[9], dev(k, s)).start()

    own_lined = group(1, own_line_got.at[pl.ds(0, Z - 1)])
    own_lined.wait_recv()
    for k in range(Z):
        own_total = own_total + own_line_got[k].astype(F32)
    tile = lax.div(own_at, TS)
    row_e = down(energy[pl.ds(2 * j + tile, 1), :], lax.rem(own_at, TS), own_piece)
    row_s = scale(2 * j + tile)
    own_rows = pl.ds(own_at, own_piece)
    for h in range(2):
        cols = slice(h * TS, (h + 1) * TS)
        col_e = energy[pl.ds(2 * j + h, 1), :]
        col_s = scale(2 * j + h)
        own_amp[own_rows, cols] = (
            own_total[:, cols] * (row_s * row_s) * col_s / (row_e + col_e)
        ).astype(BF16)
    for k in side:
        remote(own_amp.at[own_rows], own_amp.at[own_rows],
               sems.at[4], sems.at[5], dev(z, j * W + k)).start()
    own_scattered.wait_send()
    own_lined.wait_send()
    off_scattered.wait_send()

    row_e = down(energy[pl.ds(j, 1), :], w * off_piece, off_piece)
    row_s = scale(j)
    off_lined = group(4, off_line_got.at[pl.ds(0, Z - 1)])
    off_lined.wait_recv()
    for k in range(Z):
        off_total = off_total + off_line_got[k].astype(F32)
    for h in range(2):
        cols = slice(h * TS, (h + 1) * TS)
        denominator = row_e + energy[2 + h:3 + h, :]
        col_s = scale(2 + h)
        value = off_total[:, cols]
        stage[0, :, cols] = (value * (col_s * col_s) * row_s / denominator).astype(BF16)
        stage[1, :, cols] = (value * (row_s * row_s) * col_s / denominator).astype(BF16)
    off_rows = pl.ds(off_at, off_piece)
    for k in plane:
        remote(stage.at[lax.div(k, W)], off_amp.at[off_rows],
               sems.at[10], sems.at[11], dev(z, k)).start()
    send_b(1, 2).start()
    off_amp[off_rows, :] = stage[j]

    own_gathered = group(2, own_amp.at[pl.ds(0, (W - 1) * own_piece)])
    own_gathered.wait_recv()
    own_product[...] = nn_dot(b_ref[...], own_amp[...])
    own_gathered.wait_send()
    off_lined.wait_send()
    off_gathered = group(5, off_amp.at[pl.ds(0, (S - 1) * off_piece)])
    off_gathered.wait_send()
    send_b(1, 0).wait_send()
    send_b(1, 1).wait_send()
    off_gathered.wait_recv()

    def result(at):
        @pl.when(j == 0)
        def _():
            out_ref[at, :] = (own_product[at, :] + nt_dot(other[at, :], off_amp[...])).astype(BF16)

        @pl.when(j == 1)
        def _():
            out_ref[at, :] = (own_product[at, :] + nn_dot(other[at, :], off_amp[...])).astype(BF16)

    result(pl.ds(here, half))
    for p in range(3):
        got_b(1, p).wait_recv()
        if p > 0:
            start, count = parts[1][p]
            if p == 1:
                start, count = 0, parts[1][0][1] + count
            result(pl.ds(pl.multiple_of(away + start, 16), count))
    send_b(1, 2).wait_send()


def pair_body(W, Z, three_index, occupied_energy, virtual_energy, tile_occupied, tile_virtual,
              tile_exponent):
    rows, width = three_index.shape
    S = 2 * W
    own_piece = width // W
    off_piece = width // S
    half = rows // 2
    first = half // 32 * 16
    small = half // 112 * 16
    parts = (
        tuple((i * first // 2, first // 2) for i in range(4)),
        ((0, small), (small, first), (small + first, half - first - small)),
    )
    hbm = pl.BlockSpec(memory_space=pltpu.HBM)
    vmem = pl.BlockSpec(memory_space=pltpu.VMEM)
    dma = pltpu.SemaphoreType.DMA
    flops = 2 * rows * width * width
    return pl.pallas_call(
        functools.partial(kernel, W, Z, parts),
        out_shape=pltpu.VMEM((rows, width), BF16),
        in_specs=[hbm] * 6,
        out_specs=vmem,
        scratch_shapes=[
            pltpu.VMEM((rows, width), BF16),
            pltpu.VMEM((VT, TS), F32),
            pltpu.SMEM(occupied_energy.shape, F32),
            pltpu.SMEM(tile_occupied.shape, jnp.int32),
            pltpu.SMEM(tile_virtual.shape, jnp.int32),
            pltpu.SMEM(tile_exponent.shape, jnp.int32),
            pltpu.VMEM((rows, width), F32),
            pltpu.VMEM((rows, width), BF16),
            pltpu.VMEM((width, width), BF16),
            pltpu.VMEM((width, width), F32),
            pltpu.VMEM((width, width), F32),
            pltpu.VMEM((width, width), BF16),
            pltpu.VMEM((width, width), BF16),
            pltpu.VMEM((W, own_piece, width), BF16),
            pltpu.VMEM((S, off_piece, width), BF16),
            pltpu.VMEM((own_piece, width), BF16),
            pltpu.VMEM((off_piece, width), BF16),
            pltpu.VMEM((Z, own_piece, width), BF16),
            pltpu.VMEM((Z, off_piece, width), BF16),
            pltpu.VMEM((width, width), BF16),
            pltpu.VMEM((2, off_piece, width), BF16),
            pltpu.VMEM((8, TS), F32),
            dma((6,)),
            dma((7,)), dma((7,)),
            dma((12,)),
        ],
        compiler_params=pltpu.CompilerParams(
            collective_id=0, has_side_effects=True, vmem_limit_bytes=VMEM_LIMIT
        ),
        cost_estimate=pl.CostEstimate(
            flops=4 * flops, bytes_accessed=4 * rows * width, transcendentals=0
        ),
    )(three_index, virtual_energy.reshape(VT, TS), occupied_energy, tile_occupied, tile_virtual,
      tile_exponent)


def solution(mesh):
    placed = (P("aux", "pair"), P(), P(), P(), P(), P())
    W = 4
    Z = mesh.shape["aux"] // W

    def body(*args):
        if mesh.shape["pair"] == 2 and Z * W == 16 and args[0].shape[1] == 2 * TS and args[0].shape[0] % 224 == 0:
            return pair_body(W, Z, *args)
        return general_body(*args)

    return jax.shard_map(
        body, mesh=mesh, in_specs=placed, out_specs=P("aux", "pair"), check_vma=False
    )
```

```python
import functools

import jax
import jax.numpy as jnp
from jax import lax
from jax.experimental import pallas as pl
from jax.experimental.pallas import tpu as pltpu
from jax.sharding import PartitionSpec as P

TS = 128
VT = 157
F32 = jnp.float32
BF16 = jnp.bfloat16
MESH = pl.DeviceIdType.MESH
VMEM_LIMIT = 60 * 1024 * 1024


def column_scale(tile_exponent):
    factor = jnp.where(tile_exponent == -1, 0.5, jnp.where(tile_exponent == 1, 2.0, 1.0)).astype(
        jnp.float32
    )
    return jnp.repeat(factor, TS)


def column_energy(occupied_energy, virtual_energy, tile_occupied, tile_virtual):
    virtual_cols = virtual_energy.reshape(VT, TS)[tile_virtual].reshape(-1)
    occupied_cols = jnp.repeat(occupied_energy[tile_occupied], TS)
    return virtual_cols - occupied_cols


def make_amplitude(coulomb, row_energy, row_scale, own_energy, own_scale):
    return (
        coulomb
        * (row_scale * row_scale)[:, None]
        * own_scale[None, :]
        / (row_energy[:, None] + own_energy[None, :])
    ).astype(jnp.bfloat16)


def general_body(
    three_index, occupied_energy, virtual_energy, tile_occupied, tile_virtual, tile_exponent
):
    width_local = three_index.shape[1]
    col_scale = column_scale(tile_exponent)
    col_energy = column_energy(occupied_energy, virtual_energy, tile_occupied, tile_virtual)
    offset = lax.axis_index("pair") * width_local
    own_energy = lax.dynamic_slice_in_dim(col_energy, offset, width_local)
    own_scale = lax.dynamic_slice_in_dim(col_scale, offset, width_local)
    contract = (((0,), (0,)), ((), ()))
    gathered = lax.all_gather(three_index, "pair", axis=1, tiled=True)
    coulomb = lax.dot_general(gathered, three_index, contract, preferred_element_type=jnp.float32)
    summed = lax.psum(coulomb, "aux")
    amplitude = make_amplitude(summed, col_energy, col_scale, own_energy, own_scale)
    result = jnp.dot(gathered, amplitude, preferred_element_type=jnp.float32)
    return result.astype(jnp.bfloat16)


def tn_dot(a, b):
    return lax.dot_general(a, b, (((0,), (0,)), ((), ())), preferred_element_type=F32)


def nt_dot(a, b):
    return lax.dot_general(a, b, (((1,), (1,)), ((), ())), preferred_element_type=F32)


def nn_dot(a, b):
    return jnp.dot(a, b, preferred_element_type=F32)


def kernel(
    W, Z, parts, b_hbm, ve_hbm, occ_hbm, to_hbm, tv_hbm, te_hbm, out_ref,
    b_ref, ve_ref, occ_ref, to_ref, tv_ref, te_ref, own_product, other, off_amp,
    own_sum, off_sum, own_part, off_part, own_got, off_got, own_line, off_line,
    own_line_got, off_line_got, own_amp, stage, energy,
    load, b_s, b_r, sems,
):
    rows, width = b_ref.shape
    half = rows // 2
    S = 2 * W
    own_piece = width // W
    off_piece = width // S
    aux = lax.axis_index("aux")
    j = lax.axis_index("pair")
    z = lax.div(aux, W)
    w = lax.rem(aux, W)
    s = j * W + w

    def dev(line, place):
        return {"aux": line * W + lax.rem(place, W), "pair": lax.div(place, W)}

    def remote(src, dst, send, recv, target):
        return pltpu.make_async_remote_copy(
            src_ref=src, dst_ref=dst, send_sem=send, recv_sem=recv,
            device_id=target, device_id_type=MESH,
        )

    across = dev(z, lax.rem(s + W, S))
    far = [(1 - j) * W + lax.rem(w + i, W) for i in range(W)]
    near = [j * W + lax.rem(w + i, W) for i in range(1, W)]
    plane = far + near
    side = [lax.rem(w + i, W) for i in range(1, W)]
    line = [lax.rem(z + i, Z) for i in range(1, Z)]

    loads = [
        pltpu.make_async_copy(src, dst, load.at[k])
        for k, (src, dst) in enumerate([
            (b_hbm, b_ref), (ve_hbm, ve_ref), (occ_hbm, occ_ref),
            (to_hbm, to_ref), (tv_hbm, tv_ref), (te_hbm, te_ref),
        ])
    ]
    barrier = pltpu.get_barrier_semaphore()
    for k in plane:
        pl.semaphore_signal(barrier, inc=1, device_id=dev(z, k), device_id_type=MESH)
    for k in line:
        pl.semaphore_signal(barrier, inc=1, device_id=dev(k, s), device_id_type=MESH)
    for one in loads:
        one.start()

    here = pl.multiple_of((1 - j) * half, half)
    away = pl.multiple_of(j * half, half)
    own_at = pl.multiple_of(w * own_piece, own_piece)
    off_at = pl.multiple_of(s * off_piece, off_piece)

    halves = [(away, here, parts[0]), (here, away, parts[1])]

    def b_copy(src, dst, k, p):
        sem = (len(parts[0]) if k else 0) + p
        source = b_hbm if k == 0 and p == 0 else b_ref
        return remote(source.at[src], other.at[dst], b_s.at[sem], b_r.at[sem], across)

    def b_rows(first, k, p):
        start, count = parts[k][p]
        return pl.ds(pl.multiple_of(first + start, 16), count)

    def send_b(k, p):
        at = b_rows(halves[k][0], k, p)
        return b_copy(at, at, k, p)

    def got_b(k, p):
        at = b_rows(halves[k][1], k, p)
        return b_copy(at, at, k, p)

    def group(k, ref):
        return remote(ref, ref, sems.at[2 * k], sems.at[2 * k + 1], across)

    def scale(t):
        e = te_ref[t]
        return jnp.where(e == -1, 0.5, jnp.where(e == 1, 2.0, 1.0)).astype(F32)

    def down(row, first, count):
        shape = (count, TS)
        pick = lax.broadcasted_iota(jnp.int32, shape, 1) == (
            lax.broadcasted_iota(jnp.int32, shape, 0) + first)
        return jnp.sum(jnp.where(pick, row, 0.0), axis=1, keepdims=True)

    pl.semaphore_wait(barrier, S - 1 + Z - 1)
    send_b(0, 0).start()
    loads[0].wait()
    for p in range(1, len(parts[0])):
        send_b(0, p).start()

    own_sum[...] = tn_dot(b_ref[...], b_ref[...])
    own_part[...] = own_sum[...].astype(BF16)
    for k in side:
        remote(own_part.at[pl.ds(pl.multiple_of(k * own_piece, own_piece), own_piece)],
               own_got.at[w], sems.at[0], sems.at[1], dev(z, j * W + k)).start()

    for one in loads[1:]:
        one.wait()
    for t in range(4):
        energy[t:t + 1, :] = ve_ref[pl.ds(tv_ref[t], 1), :] - occ_ref[to_ref[t]]
    own_got[w] = jnp.zeros(own_got.shape[1:], BF16)
    off_got[s] = jnp.zeros(off_got.shape[1:], BF16)
    own_line_got[z] = jnp.zeros(own_line_got.shape[1:], BF16)
    off_line_got[z] = jnp.zeros(off_line_got.shape[1:], BF16)

    own_scattered = group(0, own_got.at[pl.ds(0, W - 1)])
    own_scattered.wait_recv()
    own_total = own_sum[pl.ds(own_at, own_piece), :]
    for k in range(W):
        own_total = own_total + own_got[k].astype(F32)
    own_line[...] = own_total.astype(BF16)
    for k in line:
        remote(own_line, own_line_got.at[z], sems.at[2], sems.at[3], dev(k, s)).start()

    for p in range(0, len(parts[0]), 2):
        if p == len(parts[0]) - 2:
            for sent in range(len(parts[0])):
                send_b(0, sent).wait_send()
            send_b(1, 0).start()
        got_b(0, p).wait_recv()
        got_b(0, p + 1).wait_recv()
        at = pl.ds(pl.multiple_of(here + parts[0][p][0], 16), parts[0][p][1] + parts[0][p + 1][1])

        for side_chips, first in ((far, 1 - j), (near, j)):
            cols = pl.ds(pl.multiple_of(first * TS, TS), TS)

            @pl.when(j == 0)
            def _():
                value = tn_dot(b_ref[at, cols], other[at, :])
                off_sum[cols, :] = value if p == 0 else off_sum[cols, :] + value

            @pl.when(j == 1)
            def _():
                value = tn_dot(other[at, cols], b_ref[at, :])
                off_sum[cols, :] = value if p == 0 else off_sum[cols, :] + value

            if p == len(parts[0]) - 2:
                off_part[cols, :] = off_sum[cols, :].astype(BF16)
                for k in side_chips:
                    piece = pl.ds(pl.multiple_of(k * off_piece, off_piece), off_piece)
                    remote(off_part.at[piece], off_got.at[s], sems.at[6], sems.at[7],
                           dev(z, k)).start()

    off_scattered = group(3, off_got.at[pl.ds(0, S - 1)])
    off_scattered.wait_recv()
    send_b(1, 1).start()
    off_total = off_sum[pl.ds(off_at, off_piece), :]
    for k in range(S):
        off_total = off_total + off_got[k].astype(F32)
    off_line[...] = off_total.astype(BF16)
    for k in line:
        remote(off_line, off_line_got.at[z], sems.at[8], sems.at[9], dev(k, s)).start()

    own_lined = group(1, own_line_got.at[pl.ds(0, Z - 1)])
    own_lined.wait_recv()
    for k in range(Z):
        own_total = own_total + own_line_got[k].astype(F32)
    tile = lax.div(own_at, TS)
    row_e = down(energy[pl.ds(2 * j + tile, 1), :], lax.rem(own_at, TS), own_piece)
    row_s = scale(2 * j + tile)
    own_rows = pl.ds(own_at, own_piece)
    for h in range(2):
        cols = slice(h * TS, (h + 1) * TS)
        col_e = energy[pl.ds(2 * j + h, 1), :]
        col_s = scale(2 * j + h)
        own_amp[own_rows, cols] = (
            own_total[:, cols] * (row_s * row_s) * col_s / (row_e + col_e)
        ).astype(BF16)
    for k in side:
        remote(own_amp.at[own_rows], own_amp.at[own_rows],
               sems.at[4], sems.at[5], dev(z, j * W + k)).start()
    own_scattered.wait_send()
    own_lined.wait_send()
    off_scattered.wait_send()

    row_e = down(energy[pl.ds(j, 1), :], w * off_piece, off_piece)
    row_s = scale(j)
    off_lined = group(4, off_line_got.at[pl.ds(0, Z - 1)])
    off_lined.wait_recv()
    for k in range(Z):
        off_total = off_total + off_line_got[k].astype(F32)
    for h in range(2):
        cols = slice(h * TS, (h + 1) * TS)
        denominator = row_e + energy[2 + h:3 + h, :]
        col_s = scale(2 + h)
        value = off_total[:, cols]
        stage[0, :, cols] = (value * (col_s * col_s) * row_s / denominator).astype(BF16)
        stage[1, :, cols] = (value * (row_s * row_s) * col_s / denominator).astype(BF16)
    off_rows = pl.ds(off_at, off_piece)
    for k in plane:
        remote(stage.at[lax.div(k, W)], off_amp.at[off_rows],
               sems.at[10], sems.at[11], dev(z, k)).start()
    send_b(1, 2).start()
    off_amp[off_rows, :] = stage[j]

    own_gathered = group(2, own_amp.at[pl.ds(0, (W - 1) * own_piece)])
    own_gathered.wait_recv()
    own_product[...] = nn_dot(b_ref[...], own_amp[...])
    own_gathered.wait_send()
    off_lined.wait_send()
    off_gathered = group(5, off_amp.at[pl.ds(0, (S - 1) * off_piece)])
    off_gathered.wait_send()
    send_b(1, 0).wait_send()
    send_b(1, 1).wait_send()
    off_gathered.wait_recv()

    def result(at):
        @pl.when(j == 0)
        def _():
            out_ref[at, :] = (own_product[at, :] + nt_dot(other[at, :], off_amp[...])).astype(BF16)

        @pl.when(j == 1)
        def _():
            out_ref[at, :] = (own_product[at, :] + nn_dot(other[at, :], off_amp[...])).astype(BF16)

    result(pl.ds(here, half))
    for p in range(3):
        got_b(1, p).wait_recv()
        if p > 0:
            start, count = parts[1][p]
            if p == 1:
                start, count = 0, parts[1][0][1] + count
            result(pl.ds(pl.multiple_of(away + start, 16), count))
    send_b(1, 2).wait_send()


def pair_body(W, Z, three_index, occupied_energy, virtual_energy, tile_occupied, tile_virtual,
              tile_exponent):
    rows, width = three_index.shape
    S = 2 * W
    own_piece = width // W
    off_piece = width // S
    half = rows // 2
    first = half // 32 * 16
    small = 32
    middle = 240
    parts = (
        tuple((i * first // 2, first // 2) for i in range(4)),
        ((0, small), (small, middle), (small + middle, half - middle - small)),
    )
    hbm = pl.BlockSpec(memory_space=pltpu.HBM)
    vmem = pl.BlockSpec(memory_space=pltpu.VMEM)
    dma = pltpu.SemaphoreType.DMA
    flops = 2 * rows * width * width
    return pl.pallas_call(
        functools.partial(kernel, W, Z, parts),
        out_shape=pltpu.VMEM((rows, width), BF16),
        in_specs=[hbm] * 6,
        out_specs=vmem,
        scratch_shapes=[
            pltpu.VMEM((rows, width), BF16),
            pltpu.VMEM((VT, TS), F32),
            pltpu.SMEM(occupied_energy.shape, F32),
            pltpu.SMEM(tile_occupied.shape, jnp.int32),
            pltpu.SMEM(tile_virtual.shape, jnp.int32),
            pltpu.SMEM(tile_exponent.shape, jnp.int32),
            pltpu.VMEM((rows, width), F32),
            pltpu.VMEM((rows, width), BF16),
            pltpu.VMEM((width, width), BF16),
            pltpu.VMEM((width, width), F32),
            pltpu.VMEM((width, width), F32),
            pltpu.VMEM((width, width), BF16),
            pltpu.VMEM((width, width), BF16),
            pltpu.VMEM((W, own_piece, width), BF16),
            pltpu.VMEM((S, off_piece, width), BF16),
            pltpu.VMEM((own_piece, width), BF16),
            pltpu.VMEM((off_piece, width), BF16),
            pltpu.VMEM((Z, own_piece, width), BF16),
            pltpu.VMEM((Z, off_piece, width), BF16),
            pltpu.VMEM((width, width), BF16),
            pltpu.VMEM((2, off_piece, width), BF16),
            pltpu.VMEM((8, TS), F32),
            dma((6,)),
            dma((7,)), dma((7,)),
            dma((12,)),
        ],
        compiler_params=pltpu.CompilerParams(
            collective_id=0, has_side_effects=True, vmem_limit_bytes=VMEM_LIMIT
        ),
        cost_estimate=pl.CostEstimate(
            flops=4 * flops, bytes_accessed=4 * rows * width, transcendentals=0
        ),
    )(three_index, virtual_energy.reshape(VT, TS), occupied_energy, tile_occupied, tile_virtual,
      tile_exponent)


def solution(mesh):
    placed = (P("aux", "pair"), P(), P(), P(), P(), P())
    W = 4
    Z = mesh.shape["aux"] // W

    def body(*args):
        if mesh.shape["pair"] == 2 and Z * W == 16 and args[0].shape[1] == 2 * TS and args[0].shape[0] == 896:
            return pair_body(W, Z, *args)
        return general_body(*args)

    return jax.shard_map(
        body, mesh=mesh, in_specs=placed, out_specs=P("aux", "pair"), check_vma=False
    )
```

```python
import functools

import jax
import jax.numpy as jnp
from jax import lax
from jax.experimental import pallas as pl
from jax.experimental.pallas import tpu as pltpu
from jax.sharding import PartitionSpec as P

TS = 128
VT = 157
F32 = jnp.float32
BF16 = jnp.bfloat16
MESH = pl.DeviceIdType.MESH
VMEM_LIMIT = 60 * 1024 * 1024


def column_scale(tile_exponent):
    factor = jnp.where(tile_exponent == -1, 0.5, jnp.where(tile_exponent == 1, 2.0, 1.0)).astype(
        jnp.float32
    )
    return jnp.repeat(factor, TS)


def column_energy(occupied_energy, virtual_energy, tile_occupied, tile_virtual):
    virtual_cols = virtual_energy.reshape(VT, TS)[tile_virtual].reshape(-1)
    occupied_cols = jnp.repeat(occupied_energy[tile_occupied], TS)
    return virtual_cols - occupied_cols


def make_amplitude(coulomb, row_energy, row_scale, own_energy, own_scale):
    return (
        coulomb
        * (row_scale * row_scale)[:, None]
        * own_scale[None, :]
        / (row_energy[:, None] + own_energy[None, :])
    ).astype(jnp.bfloat16)


def general_body(
    three_index, occupied_energy, virtual_energy, tile_occupied, tile_virtual, tile_exponent
):
    width_local = three_index.shape[1]
    col_scale = column_scale(tile_exponent)
    col_energy = column_energy(occupied_energy, virtual_energy, tile_occupied, tile_virtual)
    offset = lax.axis_index("pair") * width_local
    own_energy = lax.dynamic_slice_in_dim(col_energy, offset, width_local)
    own_scale = lax.dynamic_slice_in_dim(col_scale, offset, width_local)
    contract = (((0,), (0,)), ((), ()))
    gathered = lax.all_gather(three_index, "pair", axis=1, tiled=True)
    coulomb = lax.dot_general(gathered, three_index, contract, preferred_element_type=jnp.float32)
    summed = lax.psum(coulomb, "aux")
    amplitude = make_amplitude(summed, col_energy, col_scale, own_energy, own_scale)
    result = jnp.dot(gathered, amplitude, preferred_element_type=jnp.float32)
    return result.astype(jnp.bfloat16)


def tn_dot(a, b):
    return lax.dot_general(a, b, (((0,), (0,)), ((), ())), preferred_element_type=F32)


def nt_dot(a, b):
    return lax.dot_general(a, b, (((1,), (1,)), ((), ())), preferred_element_type=F32)


def nn_dot(a, b):
    return jnp.dot(a, b, preferred_element_type=F32)


def kernel(
    W, Z, parts, b_hbm, ve_hbm, occ_hbm, to_hbm, tv_hbm, te_hbm, out_ref,
    b_ref, ve_ref, occ_ref, to_ref, tv_ref, te_ref, own_product, other, off_amp,
    own_sum, off_sum, own_part, off_part, own_got, off_got, own_line, off_line,
    own_line_got, off_line_got, own_amp, stage, energy,
    load, b_s, b_r, sems,
):
    rows, width = b_ref.shape
    half = rows // 2
    S = 2 * W
    own_piece = width // W
    off_piece = width // S
    aux = lax.axis_index("aux")
    j = lax.axis_index("pair")
    z = lax.div(aux, W)
    w = lax.rem(aux, W)
    s = j * W + w

    def dev(line, place):
        return {"aux": line * W + lax.rem(place, W), "pair": lax.div(place, W)}

    def remote(src, dst, send, recv, target):
        return pltpu.make_async_remote_copy(
            src_ref=src, dst_ref=dst, send_sem=send, recv_sem=recv,
            device_id=target, device_id_type=MESH,
        )

    across = dev(z, lax.rem(s + W, S))
    plane = [lax.rem(s + i, S) for i in range(1, S)]
    side = [lax.rem(w + i, W) for i in range(1, W)]
    line = [lax.rem(z + i, Z) for i in range(1, Z)]

    loads = [
        pltpu.make_async_copy(src, dst, load.at[k])
        for k, (src, dst) in enumerate([
            (b_hbm, b_ref), (ve_hbm, ve_ref), (occ_hbm, occ_ref),
            (to_hbm, to_ref), (tv_hbm, tv_ref), (te_hbm, te_ref),
        ])
    ]
    barrier = pltpu.get_barrier_semaphore()
    for k in plane:
        pl.semaphore_signal(barrier, inc=1, device_id=dev(z, k), device_id_type=MESH)
    for k in line:
        pl.semaphore_signal(barrier, inc=1, device_id=dev(k, s), device_id_type=MESH)
    for one in loads:
        one.start()

    here = pl.multiple_of((1 - j) * half, half)
    away = pl.multiple_of(j * half, half)
    own_at = pl.multiple_of(w * own_piece, own_piece)
    off_at = pl.multiple_of(s * off_piece, off_piece)

    halves = [(away, here, parts[0]), (here, away, parts[1])]

    def b_copy(src, dst, k, p):
        sem = (len(parts[0]) if k else 0) + p
        return remote(b_ref.at[src], other.at[dst], b_s.at[sem], b_r.at[sem], across)

    def b_rows(first, k, p):
        start, count = parts[k][p]
        return pl.ds(pl.multiple_of(first + start, 16), count)

    def send_b(k, p):
        at = b_rows(halves[k][0], k, p)
        return b_copy(at, at, k, p)

    def got_b(k, p):
        at = b_rows(halves[k][1], k, p)
        return b_copy(at, at, k, p)

    def group(k, ref):
        return remote(ref, ref, sems.at[2 * k], sems.at[2 * k + 1], across)

    def scale(t):
        e = te_ref[t]
        return jnp.where(e == -1, 0.5, jnp.where(e == 1, 2.0, 1.0)).astype(F32)

    def down(row, first, count):
        shape = (count, TS)
        pick = lax.broadcasted_iota(jnp.int32, shape, 1) == (
            lax.broadcasted_iota(jnp.int32, shape, 0) + first)
        return jnp.sum(jnp.where(pick, row, 0.0), axis=1, keepdims=True)

    pl.semaphore_wait(barrier, S - 1 + Z - 1)
    loads[0].wait()
    for p in range(len(parts[0])):
        send_b(0, p).start()

    own_sum[...] = tn_dot(b_ref[...], b_ref[...])
    own_part[...] = own_sum[...].astype(BF16)
    for k in side:
        remote(own_part.at[pl.ds(pl.multiple_of(k * own_piece, own_piece), own_piece)],
               own_got.at[w], sems.at[0], sems.at[1], dev(z, j * W + k)).start()

    for one in loads[1:]:
        one.wait()
    for t in range(4):
        energy[t:t + 1, :] = ve_ref[pl.ds(tv_ref[t], 1), :] - occ_ref[to_ref[t]]
    own_got[w] = jnp.zeros(own_got.shape[1:], BF16)
    for h in range(2):
        off_got[h, s] = jnp.zeros(off_got.shape[2:], BF16)
        off_line_got[h, z] = jnp.zeros(off_line_got.shape[2:], BF16)
    own_line_got[z] = jnp.zeros(own_line_got.shape[1:], BF16)

    own_scattered = group(0, own_got.at[pl.ds(0, W - 1)])
    own_scattered.wait_recv()
    own_total = own_sum[pl.ds(own_at, own_piece), :]
    for k in range(W):
        own_total = own_total + own_got[k].astype(F32)
    own_line[...] = own_total.astype(BF16)
    for k in line:
        remote(own_line, own_line_got.at[z], sems.at[2], sems.at[3], dev(k, s)).start()

    for p in range(0, len(parts[0]), 2):
        if p == len(parts[0]) - 2:
            for sent in range(len(parts[0])):
                send_b(0, sent).wait_send()
            send_b(1, 0).start()
        got_b(0, p).wait_recv()
        got_b(0, p + 1).wait_recv()
        at = pl.ds(pl.multiple_of(here + parts[0][p][0], 16), parts[0][p][1] + parts[0][p + 1][1])

        for h in range(2):
            cols = slice(h * TS, (h + 1) * TS)

            @pl.when(j == 0)
            def _():
                value = tn_dot(b_ref[at, :], other[at, cols])
                off_sum[h] = value if p == 0 else off_sum[h] + value

            @pl.when(j == 1)
            def _():
                value = tn_dot(other[at, :], b_ref[at, cols])
                off_sum[h] = value if p == 0 else off_sum[h] + value

            if p == len(parts[0]) - 2:
                off_part[h] = off_sum[h].astype(BF16)
                for k in plane:
                    piece = pl.ds(pl.multiple_of(k * off_piece, off_piece), off_piece)
                    remote(off_part.at[h, piece], off_got.at[h, s],
                           sems.at[6 + 2 * h], sems.at[7 + 2 * h], dev(z, k)).start()

    off_scattered = [group(3 + h, off_got.at[h, pl.ds(0, S - 1)]) for h in range(2)]
    off_total = []
    for h in range(2):
        off_scattered[h].wait_recv()
        total = off_sum[h, pl.ds(off_at, off_piece), :]
        for k in range(S):
            total = total + off_got[h, k].astype(F32)
        off_total.append(total)
        off_line[h] = total.astype(BF16)
        for k in line:
            remote(off_line.at[h], off_line_got.at[h, z],
                   sems.at[10 + 2 * h], sems.at[11 + 2 * h], dev(k, s)).start()
    send_b(1, 1).start()

    own_lined = group(1, own_line_got.at[pl.ds(0, Z - 1)])
    own_lined.wait_recv()
    for k in range(Z):
        own_total = own_total + own_line_got[k].astype(F32)
    tile = lax.div(own_at, TS)
    row_e = down(energy[pl.ds(2 * j + tile, 1), :], lax.rem(own_at, TS), own_piece)
    row_s = scale(2 * j + tile)
    own_rows = pl.ds(own_at, own_piece)
    for h in range(2):
        cols = slice(h * TS, (h + 1) * TS)
        col_e = energy[pl.ds(2 * j + h, 1), :]
        col_s = scale(2 * j + h)
        own_amp[own_rows, cols] = (
            own_total[:, cols] * (row_s * row_s) * col_s / (row_e + col_e)
        ).astype(BF16)
    for k in side:
        remote(own_amp.at[own_rows], own_amp.at[own_rows],
               sems.at[4], sems.at[5], dev(z, j * W + k)).start()
    own_scattered.wait_send()
    own_lined.wait_send()
    for h in range(2):
        off_scattered[h].wait_send()

    row_e = down(energy[pl.ds(j, 1), :], w * off_piece, off_piece)
    row_s = scale(j)
    off_rows = pl.ds(off_at, off_piece)
    off_lined = [group(5 + h, off_line_got.at[h, pl.ds(0, Z - 1)]) for h in range(2)]
    for h in range(2):
        cols = slice(h * TS, (h + 1) * TS)
        off_lined[h].wait_recv()
        value = off_total[h]
        for k in range(Z):
            value = value + off_line_got[h, k].astype(F32)
        denominator = row_e + energy[2 + h:3 + h, :]
        col_s = scale(2 + h)
        stage[h, 0] = (value * (col_s * col_s) * row_s / denominator).astype(BF16)
        stage[h, 1] = (value * (row_s * row_s) * col_s / denominator).astype(BF16)
        for k in plane:
            remote(stage.at[h, lax.div(k, W)], off_amp.at[h, off_rows],
                   sems.at[14 + 2 * h], sems.at[15 + 2 * h], dev(z, k)).start()
        off_amp[h, off_rows, :] = stage[h, j]
    send_b(1, 2).start()

    own_gathered = group(2, own_amp.at[pl.ds(0, (W - 1) * own_piece)])
    own_gathered.wait_recv()
    own_product[...] = nn_dot(b_ref[...], own_amp[...])
    own_gathered.wait_send()
    off_gathered = [
        group(7 + h, off_amp.at[h, pl.ds(0, (S - 1) * off_piece)]) for h in range(2)
    ]
    for h in range(2):
        off_lined[h].wait_send()
        off_gathered[h].wait_send()
    send_b(1, 0).wait_send()
    send_b(1, 1).wait_send()
    for h in range(2):
        off_gathered[h].wait_recv()

    def result(at):
        @pl.when(j == 0)
        def _():
            out_ref[at, :] = (own_product[at, :] + nt_dot(other[at, :TS], off_amp[0])
                              + nt_dot(other[at, TS:], off_amp[1])).astype(BF16)

        @pl.when(j == 1)
        def _():
            for h in range(2):
                cols = slice(h * TS, (h + 1) * TS)
                out_ref[at, cols] = (
                    own_product[at, cols] + nn_dot(other[at, :], off_amp[h])).astype(BF16)

    result(pl.ds(here, half))
    for p in range(3):
        got_b(1, p).wait_recv()
        if p > 0:
            start, count = parts[1][p]
            if p == 1:
                start, count = 0, parts[1][0][1] + count
            result(pl.ds(pl.multiple_of(away + start, 16), count))
    send_b(1, 2).wait_send()


def pair_body(W, Z, three_index, occupied_energy, virtual_energy, tile_occupied, tile_virtual,
              tile_exponent):
    rows, width = three_index.shape
    S = 2 * W
    own_piece = width // W
    off_piece = width // S
    half = rows // 2
    first = half // 32 * 16
    small = half // 112 * 16
    parts = (
        tuple((i * first // 2, first // 2) for i in range(4)),
        ((0, small), (small, first), (small + first, half - first - small)),
    )
    hbm = pl.BlockSpec(memory_space=pltpu.HBM)
    vmem = pl.BlockSpec(memory_space=pltpu.VMEM)
    dma = pltpu.SemaphoreType.DMA
    flops = 2 * rows * width * width
    return pl.pallas_call(
        functools.partial(kernel, W, Z, parts),
        out_shape=pltpu.VMEM((rows, width), BF16),
        in_specs=[hbm] * 6,
        out_specs=vmem,
        scratch_shapes=[
            pltpu.VMEM((rows, width), BF16),
            pltpu.VMEM((VT, TS), F32),
            pltpu.SMEM(occupied_energy.shape, F32),
            pltpu.SMEM(tile_occupied.shape, jnp.int32),
            pltpu.SMEM(tile_virtual.shape, jnp.int32),
            pltpu.SMEM(tile_exponent.shape, jnp.int32),
            pltpu.VMEM((rows, width), F32),
            pltpu.VMEM((rows, width), BF16),
            pltpu.VMEM((2, width, TS), BF16),
            pltpu.VMEM((width, width), F32),
            pltpu.VMEM((2, width, TS), F32),
            pltpu.VMEM((width, width), BF16),
            pltpu.VMEM((2, width, TS), BF16),
            pltpu.VMEM((W, own_piece, width), BF16),
            pltpu.VMEM((2, S, off_piece, TS), BF16),
            pltpu.VMEM((own_piece, width), BF16),
            pltpu.VMEM((2, off_piece, TS), BF16),
            pltpu.VMEM((Z, own_piece, width), BF16),
            pltpu.VMEM((2, Z, off_piece, TS), BF16),
            pltpu.VMEM((width, width), BF16),
            pltpu.VMEM((2, 2, off_piece, TS), BF16),
            pltpu.VMEM((8, TS), F32),
            dma((6,)),
            dma((7,)), dma((7,)),
            dma((18,)),
        ],
        compiler_params=pltpu.CompilerParams(
            collective_id=0, has_side_effects=True, vmem_limit_bytes=VMEM_LIMIT
        ),
        cost_estimate=pl.CostEstimate(
            flops=4 * flops, bytes_accessed=4 * rows * width, transcendentals=0
        ),
    )(three_index, virtual_energy.reshape(VT, TS), occupied_energy, tile_occupied, tile_virtual,
      tile_exponent)


def solution(mesh):
    placed = (P("aux", "pair"), P(), P(), P(), P(), P())
    W = 4
    Z = mesh.shape["aux"] // W

    def body(*args):
        if mesh.shape["pair"] == 2 and Z * W == 16 and args[0].shape[1] == 2 * TS and args[0].shape[0] % 224 == 0:
            return pair_body(W, Z, *args)
        return general_body(*args)

    return jax.shard_map(
        body, mesh=mesh, in_specs=placed, out_specs=P("aux", "pair"), check_vma=False
    )
```

```python
import functools

import jax
import jax.numpy as jnp
from jax import lax
from jax.experimental import pallas as pl
from jax.experimental.pallas import tpu as pltpu
from jax.sharding import PartitionSpec as P

TS = 128
VT = 157
F32 = jnp.float32
BF16 = jnp.bfloat16
MESH = pl.DeviceIdType.MESH
VMEM_LIMIT = 60 * 1024 * 1024


def column_scale(tile_exponent):
    factor = jnp.where(tile_exponent == -1, 0.5, jnp.where(tile_exponent == 1, 2.0, 1.0)).astype(
        jnp.float32
    )
    return jnp.repeat(factor, TS)


def column_energy(occupied_energy, virtual_energy, tile_occupied, tile_virtual):
    virtual_cols = virtual_energy.reshape(VT, TS)[tile_virtual].reshape(-1)
    occupied_cols = jnp.repeat(occupied_energy[tile_occupied], TS)
    return virtual_cols - occupied_cols


def make_amplitude(coulomb, row_energy, row_scale, own_energy, own_scale):
    return (
        coulomb
        * (row_scale * row_scale)[:, None]
        * own_scale[None, :]
        / (row_energy[:, None] + own_energy[None, :])
    ).astype(jnp.bfloat16)


def general_body(
    three_index, occupied_energy, virtual_energy, tile_occupied, tile_virtual, tile_exponent
):
    width_local = three_index.shape[1]
    col_scale = column_scale(tile_exponent)
    col_energy = column_energy(occupied_energy, virtual_energy, tile_occupied, tile_virtual)
    offset = lax.axis_index("pair") * width_local
    own_energy = lax.dynamic_slice_in_dim(col_energy, offset, width_local)
    own_scale = lax.dynamic_slice_in_dim(col_scale, offset, width_local)
    contract = (((0,), (0,)), ((), ()))
    gathered = lax.all_gather(three_index, "pair", axis=1, tiled=True)
    coulomb = lax.dot_general(gathered, three_index, contract, preferred_element_type=jnp.float32)
    summed = lax.psum(coulomb, "aux")
    amplitude = make_amplitude(summed, col_energy, col_scale, own_energy, own_scale)
    result = jnp.dot(gathered, amplitude, preferred_element_type=jnp.float32)
    return result.astype(jnp.bfloat16)


def tn_dot(a, b):
    return lax.dot_general(a, b, (((0,), (0,)), ((), ())), preferred_element_type=F32)


def nt_dot(a, b):
    return lax.dot_general(a, b, (((1,), (1,)), ((), ())), preferred_element_type=F32)


def nn_dot(a, b):
    return jnp.dot(a, b, preferred_element_type=F32)


def kernel(
    W, Z, parts, b_hbm, ve_hbm, occ_hbm, to_hbm, tv_hbm, te_hbm, out_ref,
    b_ref, ve_ref, occ_ref, to_ref, tv_ref, te_ref, own_product, other, off_amp,
    own_sum, off_sum, own_part, off_part, own_got, off_got, own_line, off_line,
    own_line_got, off_line_got, own_amp, stage, energy,
    load, b_s, b_r, sems,
):
    rows, width = b_ref.shape
    half = rows // 2
    S = 2 * W
    own_piece = width // W
    off_piece = width // S
    aux = lax.axis_index("aux")
    j = lax.axis_index("pair")
    z = lax.div(aux, W)
    w = lax.rem(aux, W)
    s = j * W + w
    core = lax.rem(w, 2)
    u = lax.div(s, 2)

    def dev(line, place):
        return {"aux": line * W + lax.rem(place, W), "pair": lax.div(place, W)}

    def remote(src, dst, send, recv, target):
        return pltpu.make_async_remote_copy(
            src_ref=src, dst_ref=dst, send_sem=send, recv_sem=recv,
            device_id=target, device_id_type=MESH,
        )

    across = dev(z, lax.rem(s + W, S))
    plane = [lax.rem(s + i, S) for i in range(1, S)]
    sibling = dev(z, 2 * u + 1 - core)
    equal = [lax.rem(u + i, W) for i in range(1, W)]
    side = [lax.rem(w + i, W) for i in range(1, W)]
    line = [lax.rem(z + i, Z) for i in range(1, Z)]

    loads = [
        pltpu.make_async_copy(src, dst, load.at[k])
        for k, (src, dst) in enumerate([
            (b_hbm, b_ref), (ve_hbm, ve_ref), (occ_hbm, occ_ref),
            (to_hbm, to_ref), (tv_hbm, tv_ref), (te_hbm, te_ref),
        ])
    ]
    barrier = pltpu.get_barrier_semaphore()
    for k in plane:
        pl.semaphore_signal(barrier, inc=1, device_id=dev(z, k), device_id_type=MESH)
    for k in line:
        pl.semaphore_signal(barrier, inc=1, device_id=dev(k, s), device_id_type=MESH)
    for one in loads:
        one.start()

    here = pl.multiple_of((1 - j) * half, half)
    away = pl.multiple_of(j * half, half)
    own_at = pl.multiple_of(w * own_piece, own_piece)

    def piece_rows(k):
        return pl.ds(pl.multiple_of(lax.rem(k, 2) * TS + lax.div(k, 2) * off_piece, off_piece),
                     off_piece)

    off_rows = piece_rows(s)

    halves = [(away, here, parts[0]), (here, away, parts[1])]

    def b_copy(src, dst, k, p):
        sem = (len(parts[0]) if k else 0) + p
        return remote(b_ref.at[src], other.at[dst], b_s.at[sem], b_r.at[sem], across)

    def b_rows(first, k, p):
        start, count = parts[k][p]
        return pl.ds(pl.multiple_of(first + start, 16), count)

    def send_b(k, p):
        at = b_rows(halves[k][0], k, p)
        return b_copy(at, at, k, p)

    def got_b(k, p):
        at = b_rows(halves[k][1], k, p)
        return b_copy(at, at, k, p)

    def group(k, ref):
        return remote(ref, ref, sems.at[2 * k], sems.at[2 * k + 1], across)

    def scale(t):
        e = te_ref[t]
        return jnp.where(e == -1, 0.5, jnp.where(e == 1, 2.0, 1.0)).astype(F32)

    def down(row, first, count):
        shape = (count, TS)
        pick = lax.broadcasted_iota(jnp.int32, shape, 1) == (
            lax.broadcasted_iota(jnp.int32, shape, 0) + first)
        return jnp.sum(jnp.where(pick, row, 0.0), axis=1, keepdims=True)

    pl.semaphore_wait(barrier, S - 1 + Z - 1)
    loads[0].wait()
    for p in range(len(parts[0])):
        send_b(0, p).start()

    own_sum[...] = tn_dot(b_ref[...], b_ref[...])
    own_part[...] = own_sum[...].astype(BF16)
    for k in side:
        remote(own_part.at[pl.ds(pl.multiple_of(k * own_piece, own_piece), own_piece)],
               own_got.at[w], sems.at[0], sems.at[1], dev(z, j * W + k)).start()

    for one in loads[1:]:
        one.wait()
    for t in range(4):
        energy[t:t + 1, :] = ve_ref[pl.ds(tv_ref[t], 1), :] - occ_ref[to_ref[t]]
    own_got[w] = jnp.zeros(own_got.shape[1:], BF16)
    for h in range(2):
        off_got[h, s] = jnp.zeros(off_got.shape[2:], BF16)
        off_line_got[h, z] = jnp.zeros(off_line_got.shape[2:], BF16)
    own_line_got[z] = jnp.zeros(own_line_got.shape[1:], BF16)

    own_scattered = group(0, own_got.at[pl.ds(0, W - 1)])
    own_scattered.wait_recv()
    own_total = own_sum[pl.ds(own_at, own_piece), :]
    for k in range(W):
        own_total = own_total + own_got[k].astype(F32)
    own_line[...] = own_total.astype(BF16)
    for k in line:
        remote(own_line, own_line_got.at[z], sems.at[2], sems.at[3], dev(k, s)).start()

    for p in range(0, len(parts[0]), 2):
        if p == len(parts[0]) - 2:
            for sent in range(len(parts[0])):
                send_b(0, sent).wait_send()
            send_b(1, 0).start()
        got_b(0, p).wait_recv()
        got_b(0, p + 1).wait_recv()
        at = pl.ds(pl.multiple_of(here + parts[0][p][0], 16), parts[0][p][1] + parts[0][p + 1][1])

        for h in range(2):
            cols = slice(h * TS, (h + 1) * TS)

            @pl.when(j == 0)
            def _():
                value = tn_dot(b_ref[at, :], other[at, cols])
                off_sum[h] = value if p == 0 else off_sum[h] + value

            @pl.when(j == 1)
            def _():
                value = tn_dot(other[at, :], b_ref[at, cols])
                off_sum[h] = value if p == 0 else off_sum[h] + value

            if p == len(parts[0]) - 2:
                off_part[h] = off_sum[h].astype(BF16)
                for k in plane:
                    remote(off_part.at[h, piece_rows(k)], off_got.at[h, s],
                           sems.at[6 + 2 * h], sems.at[7 + 2 * h], dev(z, k)).start()

    off_scattered = [group(3 + h, off_got.at[h, pl.ds(0, S - 1)]) for h in range(2)]
    off_total = []
    for h in range(2):
        off_scattered[h].wait_recv()
        total = off_sum[h, off_rows, :]
        for k in range(S):
            total = total + off_got[h, k].astype(F32)
        off_total.append(total)
        off_line[h] = total.astype(BF16)
        for k in line:
            remote(off_line.at[h], off_line_got.at[h, z],
                   sems.at[10 + 2 * h], sems.at[11 + 2 * h], dev(k, s)).start()
    send_b(1, 1).start()

    own_lined = group(1, own_line_got.at[pl.ds(0, Z - 1)])
    own_lined.wait_recv()
    for k in range(Z):
        own_total = own_total + own_line_got[k].astype(F32)
    tile = lax.div(own_at, TS)
    row_e = down(energy[pl.ds(2 * j + tile, 1), :], lax.rem(own_at, TS), own_piece)
    row_s = scale(2 * j + tile)
    own_rows = pl.ds(own_at, own_piece)
    for h in range(2):
        cols = slice(h * TS, (h + 1) * TS)
        col_e = energy[pl.ds(2 * j + h, 1), :]
        col_s = scale(2 * j + h)
        own_amp[own_rows, cols] = (
            own_total[:, cols] * (row_s * row_s) * col_s / (row_e + col_e)
        ).astype(BF16)
    for k in side:
        remote(own_amp.at[own_rows], own_amp.at[own_rows],
               sems.at[4], sems.at[5], dev(z, j * W + k)).start()
    own_scattered.wait_send()
    own_lined.wait_send()
    for h in range(2):
        off_scattered[h].wait_send()

    row_e = down(energy[pl.ds(core, 1), :], u * off_piece, off_piece)
    row_s = scale(core)
    off_lined = [group(5 + h, off_line_got.at[h, pl.ds(0, Z - 1)]) for h in range(2)]
    for h in range(2):
        cols = slice(h * TS, (h + 1) * TS)
        off_lined[h].wait_recv()
        value = off_total[h]
        for k in range(Z):
            value = value + off_line_got[h, k].astype(F32)
        denominator = row_e + energy[2 + h:3 + h, :]
        col_s = scale(2 + h)
        stage[h, 0] = (value * (col_s * col_s) * row_s / denominator).astype(BF16)
        stage[h, 1] = (value * (row_s * row_s) * col_s / denominator).astype(BF16)
        for k in equal:
            remote(stage.at[h, lax.div(k, W // 2)], off_amp.at[h, off_rows],
                   sems.at[14 + 2 * h], sems.at[15 + 2 * h], dev(z, 2 * k + core)).start()
        off_amp[h, off_rows, :] = stage[h, j]
    send_b(1, 2).start()

    own_gathered = group(2, own_amp.at[pl.ds(0, (W - 1) * own_piece)])
    own_gathered.wait_recv()
    own_product[...] = nn_dot(b_ref[...], own_amp[...])
    own_gathered.wait_send()
    off_gathered = [
        group(7 + h, off_amp.at[h, pl.ds(0, (W - 1) * off_piece)]) for h in range(2)
    ]
    for h in range(2):
        off_lined[h].wait_send()
        off_gathered[h].wait_send()
    send_b(1, 0).wait_send()
    send_b(1, 1).wait_send()

    def forward(h, which):
        place = off_amp.at[h, pl.ds(pl.multiple_of(which * TS, TS), TS)]
        return remote(place, place, sems.at[18 + 2 * h], sems.at[19 + 2 * h], sibling)

    for h in range(2):
        off_gathered[h].wait_recv()
        forward(h, core).start()
    for h in range(2):
        forward(h, 1 - core).wait_recv()

    def result(at):
        @pl.when(j == 0)
        def _():
            out_ref[at, :] = (own_product[at, :] + nt_dot(other[at, :TS], off_amp[0])
                              + nt_dot(other[at, TS:], off_amp[1])).astype(BF16)

        @pl.when(j == 1)
        def _():
            for h in range(2):
                cols = slice(h * TS, (h + 1) * TS)
                out_ref[at, cols] = (
                    own_product[at, cols] + nn_dot(other[at, :], off_amp[h])).astype(BF16)

    result(pl.ds(here, half))
    for p in range(3):
        got_b(1, p).wait_recv()
        if p > 0:
            start, count = parts[1][p]
            if p == 1:
                start, count = 0, parts[1][0][1] + count
            result(pl.ds(pl.multiple_of(away + start, 16), count))
    send_b(1, 2).wait_send()
    for h in range(2):
        forward(h, core).wait_send()


def pair_body(W, Z, three_index, occupied_energy, virtual_energy, tile_occupied, tile_virtual,
              tile_exponent):
    rows, width = three_index.shape
    S = 2 * W
    own_piece = width // W
    off_piece = width // S
    half = rows // 2
    first = half // 32 * 16
    small = half // 112 * 16
    parts = (
        tuple((i * first // 2, first // 2) for i in range(4)),
        ((0, small), (small, first), (small + first, half - first - small)),
    )
    hbm = pl.BlockSpec(memory_space=pltpu.HBM)
    vmem = pl.BlockSpec(memory_space=pltpu.VMEM)
    dma = pltpu.SemaphoreType.DMA
    flops = 2 * rows * width * width
    return pl.pallas_call(
        functools.partial(kernel, W, Z, parts),
        out_shape=pltpu.VMEM((rows, width), BF16),
        in_specs=[hbm] * 6,
        out_specs=vmem,
        scratch_shapes=[
            pltpu.VMEM((rows, width), BF16),
            pltpu.VMEM((VT, TS), F32),
            pltpu.SMEM(occupied_energy.shape, F32),
            pltpu.SMEM(tile_occupied.shape, jnp.int32),
            pltpu.SMEM(tile_virtual.shape, jnp.int32),
            pltpu.SMEM(tile_exponent.shape, jnp.int32),
            pltpu.VMEM((rows, width), F32),
            pltpu.VMEM((rows, width), BF16),
            pltpu.VMEM((2, width, TS), BF16),
            pltpu.VMEM((width, width), F32),
            pltpu.VMEM((2, width, TS), F32),
            pltpu.VMEM((width, width), BF16),
            pltpu.VMEM((2, width, TS), BF16),
            pltpu.VMEM((W, own_piece, width), BF16),
            pltpu.VMEM((2, S, off_piece, TS), BF16),
            pltpu.VMEM((own_piece, width), BF16),
            pltpu.VMEM((2, off_piece, TS), BF16),
            pltpu.VMEM((Z, own_piece, width), BF16),
            pltpu.VMEM((2, Z, off_piece, TS), BF16),
            pltpu.VMEM((width, width), BF16),
            pltpu.VMEM((2, 2, off_piece, TS), BF16),
            pltpu.VMEM((8, TS), F32),
            dma((6,)),
            dma((7,)), dma((7,)),
            dma((22,)),
        ],
        compiler_params=pltpu.CompilerParams(
            collective_id=0, has_side_effects=True, vmem_limit_bytes=VMEM_LIMIT
        ),
        cost_estimate=pl.CostEstimate(
            flops=4 * flops, bytes_accessed=4 * rows * width, transcendentals=0
        ),
    )(three_index, virtual_energy.reshape(VT, TS), occupied_energy, tile_occupied, tile_virtual,
      tile_exponent)


def solution(mesh):
    placed = (P("aux", "pair"), P(), P(), P(), P(), P())
    W = 4
    Z = mesh.shape["aux"] // W

    def body(*args):
        if mesh.shape["pair"] == 2 and Z * W == 16 and args[0].shape[1] == 2 * TS and args[0].shape[0] % 224 == 0:
            return pair_body(W, Z, *args)
        return general_body(*args)

    return jax.shard_map(
        body, mesh=mesh, in_specs=placed, out_specs=P("aux", "pair"), check_vma=False
    )
```

```python
import functools

import jax
import jax.numpy as jnp
from jax import lax
from jax.experimental import pallas as pl
from jax.experimental.pallas import tpu as pltpu
from jax.sharding import PartitionSpec as P

TS = 128
VT = 157
F32 = jnp.float32
BF16 = jnp.bfloat16
MESH = pl.DeviceIdType.MESH
VMEM_LIMIT = 60 * 1024 * 1024


def column_scale(tile_exponent):
    factor = jnp.where(tile_exponent == -1, 0.5, jnp.where(tile_exponent == 1, 2.0, 1.0)).astype(
        jnp.float32
    )
    return jnp.repeat(factor, TS)


def column_energy(occupied_energy, virtual_energy, tile_occupied, tile_virtual):
    virtual_cols = virtual_energy.reshape(VT, TS)[tile_virtual].reshape(-1)
    occupied_cols = jnp.repeat(occupied_energy[tile_occupied], TS)
    return virtual_cols - occupied_cols


def make_amplitude(coulomb, row_energy, row_scale, own_energy, own_scale):
    return (
        coulomb
        * (row_scale * row_scale)[:, None]
        * own_scale[None, :]
        / (row_energy[:, None] + own_energy[None, :])
    ).astype(jnp.bfloat16)


def general_body(
    three_index, occupied_energy, virtual_energy, tile_occupied, tile_virtual, tile_exponent
):
    width_local = three_index.shape[1]
    col_scale = column_scale(tile_exponent)
    col_energy = column_energy(occupied_energy, virtual_energy, tile_occupied, tile_virtual)
    offset = lax.axis_index("pair") * width_local
    own_energy = lax.dynamic_slice_in_dim(col_energy, offset, width_local)
    own_scale = lax.dynamic_slice_in_dim(col_scale, offset, width_local)
    contract = (((0,), (0,)), ((), ()))
    gathered = lax.all_gather(three_index, "pair", axis=1, tiled=True)
    coulomb = lax.dot_general(gathered, three_index, contract, preferred_element_type=jnp.float32)
    summed = lax.psum(coulomb, "aux")
    amplitude = make_amplitude(summed, col_energy, col_scale, own_energy, own_scale)
    result = jnp.dot(gathered, amplitude, preferred_element_type=jnp.float32)
    return result.astype(jnp.bfloat16)


def tn_dot(a, b):
    return lax.dot_general(a, b, (((0,), (0,)), ((), ())), preferred_element_type=F32)


def nt_dot(a, b):
    return lax.dot_general(a, b, (((1,), (1,)), ((), ())), preferred_element_type=F32)


def nn_dot(a, b):
    return jnp.dot(a, b, preferred_element_type=F32)


def kernel(
    W, Z, parts, b_hbm, ve_hbm, occ_hbm, to_hbm, tv_hbm, te_hbm, out_ref,
    b_ref, ve_ref, occ_ref, to_ref, tv_ref, te_ref, own_product, other, off_amp,
    own_sum, off_sum, own_part, off_part, own_got, off_got, own_line, off_line,
    own_line_got, off_line_got, own_amp, stage, energy,
    load, b_s, b_r, sems,
):
    rows, width = b_ref.shape
    half = rows // 2
    S = 2 * W
    own_piece = width // W
    off_piece = width // S
    aux = lax.axis_index("aux")
    j = lax.axis_index("pair")
    z = lax.div(aux, W)
    w = lax.rem(aux, W)
    s = j * W + w

    def dev(line, place):
        return {"aux": line * W + lax.rem(place, W), "pair": lax.div(place, W)}

    def remote(src, dst, send, recv, target):
        return pltpu.make_async_remote_copy(
            src_ref=src, dst_ref=dst, send_sem=send, recv_sem=recv,
            device_id=target, device_id_type=MESH,
        )

    across = dev(z, lax.rem(s + W, S))
    plane = [lax.rem(s + i, S) for i in range(1, S)]
    side = [lax.rem(w + i, W) for i in range(1, W)]
    line = [lax.rem(z + i, Z) for i in range(1, Z)]

    loads = [
        pltpu.make_async_copy(src, dst, load.at[k])
        for k, (src, dst) in enumerate([
            (b_hbm, b_ref), (ve_hbm, ve_ref), (occ_hbm, occ_ref),
            (to_hbm, to_ref), (tv_hbm, tv_ref), (te_hbm, te_ref),
        ])
    ]
    barrier = pltpu.get_barrier_semaphore()
    for k in plane:
        pl.semaphore_signal(barrier, inc=1, device_id=dev(z, k), device_id_type=MESH)
    for k in line:
        pl.semaphore_signal(barrier, inc=1, device_id=dev(k, s), device_id_type=MESH)
    for one in loads:
        one.start()

    here = pl.multiple_of((1 - j) * half, half)
    away = pl.multiple_of(j * half, half)
    own_at = pl.multiple_of(w * own_piece, own_piece)
    off_at = pl.multiple_of(s * off_piece, off_piece)

    halves = [(away, here, parts[0]), (here, away, parts[1])]

    def b_copy(src, dst, k, p):
        sem = (len(parts[0]) if k else 0) + p
        return remote(b_ref.at[src], other.at[dst], b_s.at[sem], b_r.at[sem], across)

    def b_rows(first, k, p):
        start, count = parts[k][p]
        return pl.ds(pl.multiple_of(first + start, 16), count)

    def send_b(k, p):
        at = b_rows(halves[k][0], k, p)
        return b_copy(at, at, k, p)

    def got_b(k, p):
        at = b_rows(halves[k][1], k, p)
        return b_copy(at, at, k, p)

    def group(k, ref):
        return remote(ref, ref, sems.at[2 * k], sems.at[2 * k + 1], across)

    def scale(t):
        e = te_ref[t]
        return jnp.where(e == -1, 0.5, jnp.where(e == 1, 2.0, 1.0)).astype(F32)

    def down(row, first, count):
        shape = (count, TS)
        pick = lax.broadcasted_iota(jnp.int32, shape, 1) == (
            lax.broadcasted_iota(jnp.int32, shape, 0) + first)
        return jnp.sum(jnp.where(pick, row, 0.0), axis=1, keepdims=True)

    pl.semaphore_wait(barrier, S - 1 + Z - 1)
    loads[0].wait()
    for p in range(len(parts[0])):
        send_b(0, p).start()

    own_sum[...] = tn_dot(b_ref[...], b_ref[...])
    own_part[...] = own_sum[...].astype(BF16)
    for k in side:
        remote(own_part.at[pl.ds(pl.multiple_of(k * own_piece, own_piece), own_piece)],
               own_got.at[w], sems.at[0], sems.at[1], dev(z, j * W + k)).start()

    for one in loads[1:]:
        one.wait()
    for t in range(4):
        energy[t:t + 1, :] = ve_ref[pl.ds(tv_ref[t], 1), :] - occ_ref[to_ref[t]]
    own_got[w] = jnp.zeros(own_got.shape[1:], BF16)
    for h in range(2):
        off_got[h, s] = jnp.zeros(off_got.shape[2:], BF16)
        off_line_got[h, z] = jnp.zeros(off_line_got.shape[2:], BF16)
    own_line_got[z] = jnp.zeros(own_line_got.shape[1:], BF16)

    own_scattered = group(0, own_got.at[pl.ds(0, W - 1)])
    own_scattered.wait_recv()
    own_total = own_sum[pl.ds(own_at, own_piece), :]
    for k in range(W):
        own_total = own_total + own_got[k].astype(F32)
    own_line[...] = own_total.astype(BF16)
    for k in line:
        remote(own_line, own_line_got.at[z], sems.at[2], sems.at[3], dev(k, s)).start()

    for p in range(0, len(parts[0]), 2):
        if p == len(parts[0]) - 2:
            for sent in range(len(parts[0])):
                send_b(0, sent).wait_send()
            send_b(1, 0).start()
        got_b(0, p).wait_recv()
        got_b(0, p + 1).wait_recv()
        at = pl.ds(pl.multiple_of(here + parts[0][p][0], 16), parts[0][p][1] + parts[0][p + 1][1])

        for h in range(2):
            cols = slice(h * TS, (h + 1) * TS)

            @pl.when(j == 0)
            def _():
                value = tn_dot(b_ref[at, :], other[at, cols])
                off_sum[h] = value if p == 0 else off_sum[h] + value

            @pl.when(j == 1)
            def _():
                value = tn_dot(other[at, :], b_ref[at, cols])
                off_sum[h] = value if p == 0 else off_sum[h] + value

            if p == len(parts[0]) - 2:
                off_part[h] = off_sum[h].astype(BF16)
                for k in plane:
                    piece = pl.ds(pl.multiple_of(k * off_piece, off_piece), off_piece)
                    remote(off_part.at[h, piece], off_got.at[h, s],
                           sems.at[6 + 2 * h], sems.at[7 + 2 * h], dev(z, k)).start()

    off_scattered = [group(3 + h, off_got.at[h, pl.ds(0, S - 1)]) for h in range(2)]
    for h in range(2):
        off_scattered[h].wait_send()
    send_b(1, 1).start()
    off_total = []
    for h in range(2):
        off_scattered[h].wait_recv()
        total = off_sum[h, pl.ds(off_at, off_piece), :]
        for k in range(S):
            total = total + off_got[h, k].astype(F32)
        off_total.append(total)
        off_line[h] = total.astype(BF16)
        for k in line:
            remote(off_line.at[h], off_line_got.at[h, z],
                   sems.at[10 + 2 * h], sems.at[11 + 2 * h], dev(k, s)).start()

    own_lined = group(1, own_line_got.at[pl.ds(0, Z - 1)])
    own_lined.wait_recv()
    for k in range(Z):
        own_total = own_total + own_line_got[k].astype(F32)
    tile = lax.div(own_at, TS)
    row_e = down(energy[pl.ds(2 * j + tile, 1), :], lax.rem(own_at, TS), own_piece)
    row_s = scale(2 * j + tile)
    own_rows = pl.ds(own_at, own_piece)
    for h in range(2):
        cols = slice(h * TS, (h + 1) * TS)
        col_e = energy[pl.ds(2 * j + h, 1), :]
        col_s = scale(2 * j + h)
        own_amp[own_rows, cols] = (
            own_total[:, cols] * (row_s * row_s) * col_s / (row_e + col_e)
        ).astype(BF16)
    for k in side:
        remote(own_amp.at[own_rows], own_amp.at[own_rows],
               sems.at[4], sems.at[5], dev(z, j * W + k)).start()
    own_scattered.wait_send()
    own_lined.wait_send()

    row_e = down(energy[pl.ds(j, 1), :], w * off_piece, off_piece)
    row_s = scale(j)
    off_rows = pl.ds(off_at, off_piece)
    off_lined = [group(5 + h, off_line_got.at[h, pl.ds(0, Z - 1)]) for h in range(2)]
    for h in range(2):
        cols = slice(h * TS, (h + 1) * TS)
        off_lined[h].wait_recv()
        value = off_total[h]
        for k in range(Z):
            value = value + off_line_got[h, k].astype(F32)
        denominator = row_e + energy[2 + h:3 + h, :]
        col_s = scale(2 + h)
        stage[h, 0] = (value * (col_s * col_s) * row_s / denominator).astype(BF16)
        stage[h, 1] = (value * (row_s * row_s) * col_s / denominator).astype(BF16)
        for k in plane:
            remote(stage.at[h, lax.div(k, W)], off_amp.at[h, off_rows],
                   sems.at[14 + 2 * h], sems.at[15 + 2 * h], dev(z, k)).start()
        off_amp[h, off_rows, :] = stage[h, j]
    send_b(1, 2).start()

    own_gathered = group(2, own_amp.at[pl.ds(0, (W - 1) * own_piece)])
    own_gathered.wait_recv()
    own_product[...] = nn_dot(b_ref[...], own_amp[...])
    own_gathered.wait_send()
    off_gathered = [
        group(7 + h, off_amp.at[h, pl.ds(0, (S - 1) * off_piece)]) for h in range(2)
    ]
    for h in range(2):
        off_lined[h].wait_send()
        off_gathered[h].wait_send()
    send_b(1, 0).wait_send()
    send_b(1, 1).wait_send()
    for h in range(2):
        off_gathered[h].wait_recv()

    def result(at):
        @pl.when(j == 0)
        def _():
            out_ref[at, :] = (own_product[at, :] + nt_dot(other[at, :TS], off_amp[0])
                              + nt_dot(other[at, TS:], off_amp[1])).astype(BF16)

        @pl.when(j == 1)
        def _():
            for h in range(2):
                cols = slice(h * TS, (h + 1) * TS)
                out_ref[at, cols] = (
                    own_product[at, cols] + nn_dot(other[at, :], off_amp[h])).astype(BF16)

    result(pl.ds(here, half))
    for p in range(3):
        got_b(1, p).wait_recv()
        if p > 0:
            start, count = parts[1][p]
            if p == 1:
                start, count = 0, parts[1][0][1] + count
            result(pl.ds(pl.multiple_of(away + start, 16), count))
    send_b(1, 2).wait_send()


def pair_body(W, Z, three_index, occupied_energy, virtual_energy, tile_occupied, tile_virtual,
              tile_exponent):
    rows, width = three_index.shape
    S = 2 * W
    own_piece = width // W
    off_piece = width // S
    half = rows // 2
    first = half // 32 * 16
    small = half // 112 * 16
    middle = half // 28 * 16 + 16
    parts = (
        tuple((i * first // 2, first // 2) for i in range(4)),
        ((0, small), (small, middle), (small + middle, half - middle - small)),
    )
    hbm = pl.BlockSpec(memory_space=pltpu.HBM)
    vmem = pl.BlockSpec(memory_space=pltpu.VMEM)
    dma = pltpu.SemaphoreType.DMA
    flops = 2 * rows * width * width
    return pl.pallas_call(
        functools.partial(kernel, W, Z, parts),
        out_shape=pltpu.VMEM((rows, width), BF16),
        in_specs=[hbm] * 6,
        out_specs=vmem,
        scratch_shapes=[
            pltpu.VMEM((rows, width), BF16),
            pltpu.VMEM((VT, TS), F32),
            pltpu.SMEM(occupied_energy.shape, F32),
            pltpu.SMEM(tile_occupied.shape, jnp.int32),
            pltpu.SMEM(tile_virtual.shape, jnp.int32),
            pltpu.SMEM(tile_exponent.shape, jnp.int32),
            pltpu.VMEM((rows, width), F32),
            pltpu.VMEM((rows, width), BF16),
            pltpu.VMEM((2, width, TS), BF16),
            pltpu.VMEM((width, width), F32),
            pltpu.VMEM((2, width, TS), F32),
            pltpu.VMEM((width, width), BF16),
            pltpu.VMEM((2, width, TS), BF16),
            pltpu.VMEM((W, own_piece, width), BF16),
            pltpu.VMEM((2, S, off_piece, TS), BF16),
            pltpu.VMEM((own_piece, width), BF16),
            pltpu.VMEM((2, off_piece, TS), BF16),
            pltpu.VMEM((Z, own_piece, width), BF16),
            pltpu.VMEM((2, Z, off_piece, TS), BF16),
            pltpu.VMEM((width, width), BF16),
            pltpu.VMEM((2, 2, off_piece, TS), BF16),
            pltpu.VMEM((8, TS), F32),
            dma((6,)),
            dma((7,)), dma((7,)),
            dma((18,)),
        ],
        compiler_params=pltpu.CompilerParams(
            collective_id=0, has_side_effects=True, vmem_limit_bytes=VMEM_LIMIT
        ),
        cost_estimate=pl.CostEstimate(
            flops=4 * flops, bytes_accessed=4 * rows * width, transcendentals=0
        ),
    )(three_index, virtual_energy.reshape(VT, TS), occupied_energy, tile_occupied, tile_virtual,
      tile_exponent)


def solution(mesh):
    placed = (P("aux", "pair"), P(), P(), P(), P(), P())
    W = 4
    Z = mesh.shape["aux"] // W

    def body(*args):
        if mesh.shape["pair"] == 2 and Z * W == 16 and args[0].shape[1] == 2 * TS and args[0].shape[0] % 224 == 0:
            return pair_body(W, Z, *args)
        return general_body(*args)

    return jax.shard_map(
        body, mesh=mesh, in_specs=placed, out_specs=P("aux", "pair"), check_vma=False
    )
```

```python
import functools

import jax
import jax.numpy as jnp
from jax import lax
from jax.experimental import pallas as pl
from jax.experimental.pallas import tpu as pltpu
from jax.sharding import PartitionSpec as P

TS = 128
VT = 157
F32 = jnp.float32
BF16 = jnp.bfloat16
MESH = pl.DeviceIdType.MESH
VMEM_LIMIT = 60 * 1024 * 1024


def column_scale(tile_exponent):
    factor = jnp.where(tile_exponent == -1, 0.5, jnp.where(tile_exponent == 1, 2.0, 1.0)).astype(
        jnp.float32
    )
    return jnp.repeat(factor, TS)


def column_energy(occupied_energy, virtual_energy, tile_occupied, tile_virtual):
    virtual_cols = virtual_energy.reshape(VT, TS)[tile_virtual].reshape(-1)
    occupied_cols = jnp.repeat(occupied_energy[tile_occupied], TS)
    return virtual_cols - occupied_cols


def make_amplitude(coulomb, row_energy, row_scale, own_energy, own_scale):
    return (
        coulomb
        * (row_scale * row_scale)[:, None]
        * own_scale[None, :]
        / (row_energy[:, None] + own_energy[None, :])
    ).astype(jnp.bfloat16)


def general_body(
    three_index, occupied_energy, virtual_energy, tile_occupied, tile_virtual, tile_exponent
):
    width_local = three_index.shape[1]
    col_scale = column_scale(tile_exponent)
    col_energy = column_energy(occupied_energy, virtual_energy, tile_occupied, tile_virtual)
    offset = lax.axis_index("pair") * width_local
    own_energy = lax.dynamic_slice_in_dim(col_energy, offset, width_local)
    own_scale = lax.dynamic_slice_in_dim(col_scale, offset, width_local)
    contract = (((0,), (0,)), ((), ()))
    gathered = lax.all_gather(three_index, "pair", axis=1, tiled=True)
    coulomb = lax.dot_general(gathered, three_index, contract, preferred_element_type=jnp.float32)
    summed = lax.psum(coulomb, "aux")
    amplitude = make_amplitude(summed, col_energy, col_scale, own_energy, own_scale)
    result = jnp.dot(gathered, amplitude, preferred_element_type=jnp.float32)
    return result.astype(jnp.bfloat16)


def tn_dot(a, b):
    return lax.dot_general(a, b, (((0,), (0,)), ((), ())), preferred_element_type=F32)


def nt_dot(a, b):
    return lax.dot_general(a, b, (((1,), (1,)), ((), ())), preferred_element_type=F32)


def nn_dot(a, b):
    return jnp.dot(a, b, preferred_element_type=F32)


def kernel(
    W, Z, parts, b_hbm, ve_hbm, occ_hbm, to_hbm, tv_hbm, te_hbm, out_ref,
    b_ref, ve_ref, occ_ref, to_ref, tv_ref, te_ref, own_product, other, off_amp,
    own_sum, off_sum, own_part, off_part, own_got, off_got, own_line, off_line,
    own_line_got, off_line_got, own_amp, stage, energy,
    load, b_s, b_r, sems,
):
    rows, width = b_ref.shape
    half = rows // 2
    S = 2 * W
    own_piece = width // W
    off_piece = width // S
    aux = lax.axis_index("aux")
    j = lax.axis_index("pair")
    z = lax.div(aux, W)
    w = lax.rem(aux, W)
    s = j * W + w

    def dev(line, place):
        return {"aux": line * W + lax.rem(place, W), "pair": lax.div(place, W)}

    def remote(src, dst, send, recv, target):
        return pltpu.make_async_remote_copy(
            src_ref=src, dst_ref=dst, send_sem=send, recv_sem=recv,
            device_id=target, device_id_type=MESH,
        )

    across = dev(z, lax.rem(s + W, S))
    plane = [lax.rem(s + i, S) for i in range(1, S)]
    side = [lax.rem(w + i, W) for i in range(1, W)]
    line = [lax.rem(z + i, Z) for i in range(1, Z)]

    loads = [
        pltpu.make_async_copy(src, dst, load.at[k])
        for k, (src, dst) in enumerate([
            (b_hbm, b_ref), (ve_hbm, ve_ref), (occ_hbm, occ_ref),
            (to_hbm, to_ref), (tv_hbm, tv_ref), (te_hbm, te_ref),
        ])
    ]
    barrier = pltpu.get_barrier_semaphore()
    for k in plane:
        pl.semaphore_signal(barrier, inc=1, device_id=dev(z, k), device_id_type=MESH)
    for k in line:
        pl.semaphore_signal(barrier, inc=1, device_id=dev(k, s), device_id_type=MESH)
    for one in loads:
        one.start()

    here = pl.multiple_of((1 - j) * half, half)
    away = pl.multiple_of(j * half, half)
    own_at = pl.multiple_of(w * own_piece, own_piece)
    off_at = pl.multiple_of(s * off_piece, off_piece)

    halves = [(away, here, parts[0]), (here, away, parts[1])]

    def b_copy(src, dst, k, p):
        sem = (len(parts[0]) if k else 0) + p
        return remote(b_ref.at[src], other.at[dst], b_s.at[sem], b_r.at[sem], across)

    def b_rows(first, k, p):
        start, count = parts[k][p]
        return pl.ds(pl.multiple_of(first + start, 16), count)

    def send_b(k, p):
        at = b_rows(halves[k][0], k, p)
        return b_copy(at, at, k, p)

    def got_b(k, p):
        at = b_rows(halves[k][1], k, p)
        return b_copy(at, at, k, p)

    def group(k, ref):
        return remote(ref, ref, sems.at[2 * k], sems.at[2 * k + 1], across)

    def scale(t):
        e = te_ref[t]
        return jnp.where(e == -1, 0.5, jnp.where(e == 1, 2.0, 1.0)).astype(F32)

    def down(row, first, count):
        shape = (count, TS)
        pick = lax.broadcasted_iota(jnp.int32, shape, 1) == (
            lax.broadcasted_iota(jnp.int32, shape, 0) + first)
        return jnp.sum(jnp.where(pick, row, 0.0), axis=1, keepdims=True)

    pl.semaphore_wait(barrier, S - 1 + Z - 1)
    loads[0].wait()
    for p in range(len(parts[0])):
        send_b(0, p).start()

    own_sum[...] = tn_dot(b_ref[...], b_ref[...])
    own_part[...] = own_sum[...].astype(BF16)
    for k in side:
        remote(own_part.at[pl.ds(pl.multiple_of(k * own_piece, own_piece), own_piece)],
               own_got.at[w], sems.at[0], sems.at[1], dev(z, j * W + k)).start()

    for one in loads[1:]:
        one.wait()
    for t in range(4):
        energy[t:t + 1, :] = ve_ref[pl.ds(tv_ref[t], 1), :] - occ_ref[to_ref[t]]
    own_got[w] = jnp.zeros(own_got.shape[1:], BF16)
    for h in range(2):
        off_got[h, s] = jnp.zeros(off_got.shape[2:], BF16)
        off_line_got[h, z] = jnp.zeros(off_line_got.shape[2:], BF16)
    own_line_got[z] = jnp.zeros(own_line_got.shape[1:], BF16)

    own_scattered = group(0, own_got.at[pl.ds(0, W - 1)])
    own_scattered.wait_recv()
    own_total = own_sum[pl.ds(own_at, own_piece), :]
    for k in range(W):
        own_total = own_total + own_got[k].astype(F32)
    own_line[...] = own_total.astype(BF16)
    for k in line:
        remote(own_line, own_line_got.at[z], sems.at[2], sems.at[3], dev(k, s)).start()

    for p in range(0, len(parts[0]), 2):
        if p == len(parts[0]) - 2:
            for sent in range(len(parts[0])):
                send_b(0, sent).wait_send()
            send_b(1, 0).start()
        got_b(0, p).wait_recv()
        got_b(0, p + 1).wait_recv()
        at = pl.ds(pl.multiple_of(here + parts[0][p][0], 16), parts[0][p][1] + parts[0][p + 1][1])

        for h in range(2):
            cols = slice(h * TS, (h + 1) * TS)

            @pl.when(j == 0)
            def _():
                value = tn_dot(b_ref[at, :], other[at, cols])
                off_sum[h] = value if p == 0 else off_sum[h] + value

            @pl.when(j == 1)
            def _():
                value = tn_dot(other[at, :], b_ref[at, cols])
                off_sum[h] = value if p == 0 else off_sum[h] + value

            if p == len(parts[0]) - 2:
                off_part[h] = off_sum[h].astype(BF16)
                for k in plane:
                    piece = pl.ds(pl.multiple_of(k * off_piece, off_piece), off_piece)
                    remote(off_part.at[h, piece], off_got.at[h, s],
                           sems.at[6 + 2 * h], sems.at[7 + 2 * h], dev(z, k)).start()

    off_scattered = [group(3 + h, off_got.at[h, pl.ds(0, S - 1)]) for h in range(2)]
    for h in range(2):
        off_scattered[h].wait_send()
    send_b(1, 1).start()
    off_total = []
    for h in range(2):
        off_scattered[h].wait_recv()
        total = off_sum[h, pl.ds(off_at, off_piece), :]
        for k in range(S):
            total = total + off_got[h, k].astype(F32)
        off_total.append(total)
        off_line[h] = total.astype(BF16)
        for k in line:
            remote(off_line.at[h], off_line_got.at[h, z],
                   sems.at[10 + 2 * h], sems.at[11 + 2 * h], dev(k, s)).start()

    own_lined = group(1, own_line_got.at[pl.ds(0, Z - 1)])
    own_lined.wait_recv()
    for k in range(Z):
        own_total = own_total + own_line_got[k].astype(F32)
    tile = lax.div(own_at, TS)
    row_e = down(energy[pl.ds(2 * j + tile, 1), :], lax.rem(own_at, TS), own_piece)
    row_s = scale(2 * j + tile)
    own_rows = pl.ds(own_at, own_piece)
    for h in range(2):
        cols = slice(h * TS, (h + 1) * TS)
        col_e = energy[pl.ds(2 * j + h, 1), :]
        col_s = scale(2 * j + h)
        own_amp[own_rows, cols] = (
            own_total[:, cols] * (row_s * row_s) * col_s / (row_e + col_e)
        ).astype(BF16)
    for k in side:
        remote(own_amp.at[own_rows], own_amp.at[own_rows],
               sems.at[4], sems.at[5], dev(z, j * W + k)).start()
    own_scattered.wait_send()
    own_lined.wait_send()

    row_e = down(energy[pl.ds(j, 1), :], w * off_piece, off_piece)
    row_s = scale(j)
    off_rows = pl.ds(off_at, off_piece)
    off_lined = [group(5 + h, off_line_got.at[h, pl.ds(0, Z - 1)]) for h in range(2)]
    for h in range(2):
        cols = slice(h * TS, (h + 1) * TS)
        off_lined[h].wait_recv()
        value = off_total[h]
        for k in range(Z):
            value = value + off_line_got[h, k].astype(F32)
        denominator = row_e + energy[2 + h:3 + h, :]
        col_s = scale(2 + h)
        stage[h, 0] = (value * (col_s * col_s) * row_s / denominator).astype(BF16)
        stage[h, 1] = (value * (row_s * row_s) * col_s / denominator).astype(BF16)
        for k in plane:
            remote(stage.at[h, lax.div(k, W)], off_amp.at[h, off_rows],
                   sems.at[14 + 2 * h], sems.at[15 + 2 * h], dev(z, k)).start()
        off_amp[h, off_rows, :] = stage[h, j]
    send_b(1, 2).start()

    own_gathered = group(2, own_amp.at[pl.ds(0, (W - 1) * own_piece)])
    own_gathered.wait_recv()
    own_product[...] = nn_dot(b_ref[...], own_amp[...])
    own_gathered.wait_send()
    off_gathered = [
        group(7 + h, off_amp.at[h, pl.ds(0, (S - 1) * off_piece)]) for h in range(2)
    ]
    for h in range(2):
        off_lined[h].wait_send()
        off_gathered[h].wait_send()
    send_b(1, 0).wait_send()
    send_b(1, 1).wait_send()
    for h in range(2):
        off_gathered[h].wait_recv()

    def result(at):
        @pl.when(j == 0)
        def _():
            out_ref[at, :] = (own_product[at, :] + nt_dot(other[at, :TS], off_amp[0])
                              + nt_dot(other[at, TS:], off_amp[1])).astype(BF16)

        @pl.when(j == 1)
        def _():
            for h in range(2):
                cols = slice(h * TS, (h + 1) * TS)
                out_ref[at, cols] = (
                    own_product[at, cols] + nn_dot(other[at, :], off_amp[h])).astype(BF16)

    result(pl.ds(here, half))
    for p in range(3):
        got_b(1, p).wait_recv()
        if p > 0:
            start, count = parts[1][p]
            if p == 1:
                start, count = 0, parts[1][0][1] + count
            result(pl.ds(pl.multiple_of(away + start, 16), count))
    send_b(1, 2).wait_send()


def pair_body(W, Z, three_index, occupied_energy, virtual_energy, tile_occupied, tile_virtual,
              tile_exponent):
    rows, width = three_index.shape
    S = 2 * W
    own_piece = width // W
    off_piece = width // S
    half = rows // 2
    first = half // 32 * 16
    small = half // 112 * 16
    middle = half // 28 * 16 + 80
    parts = (
        tuple((i * first // 2, first // 2) for i in range(4)),
        ((0, small), (small, middle), (small + middle, half - middle - small)),
    )
    hbm = pl.BlockSpec(memory_space=pltpu.HBM)
    vmem = pl.BlockSpec(memory_space=pltpu.VMEM)
    dma = pltpu.SemaphoreType.DMA
    flops = 2 * rows * width * width
    return pl.pallas_call(
        functools.partial(kernel, W, Z, parts),
        out_shape=pltpu.VMEM((rows, width), BF16),
        in_specs=[hbm] * 6,
        out_specs=vmem,
        scratch_shapes=[
            pltpu.VMEM((rows, width), BF16),
            pltpu.VMEM((VT, TS), F32),
            pltpu.SMEM(occupied_energy.shape, F32),
            pltpu.SMEM(tile_occupied.shape, jnp.int32),
            pltpu.SMEM(tile_virtual.shape, jnp.int32),
            pltpu.SMEM(tile_exponent.shape, jnp.int32),
            pltpu.VMEM((rows, width), F32),
            pltpu.VMEM((rows, width), BF16),
            pltpu.VMEM((2, width, TS), BF16),
            pltpu.VMEM((width, width), F32),
            pltpu.VMEM((2, width, TS), F32),
            pltpu.VMEM((width, width), BF16),
            pltpu.VMEM((2, width, TS), BF16),
            pltpu.VMEM((W, own_piece, width), BF16),
            pltpu.VMEM((2, S, off_piece, TS), BF16),
            pltpu.VMEM((own_piece, width), BF16),
            pltpu.VMEM((2, off_piece, TS), BF16),
            pltpu.VMEM((Z, own_piece, width), BF16),
            pltpu.VMEM((2, Z, off_piece, TS), BF16),
            pltpu.VMEM((width, width), BF16),
            pltpu.VMEM((2, 2, off_piece, TS), BF16),
            pltpu.VMEM((8, TS), F32),
            dma((6,)),
            dma((7,)), dma((7,)),
            dma((18,)),
        ],
        compiler_params=pltpu.CompilerParams(
            collective_id=0, has_side_effects=True, vmem_limit_bytes=VMEM_LIMIT
        ),
        cost_estimate=pl.CostEstimate(
            flops=4 * flops, bytes_accessed=4 * rows * width, transcendentals=0
        ),
    )(three_index, virtual_energy.reshape(VT, TS), occupied_energy, tile_occupied, tile_virtual,
      tile_exponent)


def solution(mesh):
    placed = (P("aux", "pair"), P(), P(), P(), P(), P())
    W = 4
    Z = mesh.shape["aux"] // W

    def body(*args):
        if mesh.shape["pair"] == 2 and Z * W == 16 and args[0].shape[1] == 2 * TS and args[0].shape[0] % 224 == 0:
            return pair_body(W, Z, *args)
        return general_body(*args)

    return jax.shard_map(
        body, mesh=mesh, in_specs=placed, out_specs=P("aux", "pair"), check_vma=False
    )
```
